32 devices in a mesh: depth: 4 (over y, core), freq: 8 (over z, x).
Axes of the slice: x: 2, y: 2, z: 4, core: 2. Of those that a mesh axis runs over, the one named last changes fastest.
Arguments:
- surface: float32 [64, 2, 64, 256], P('freq'), may hold values from -6 to 6
- freq_slot: int32 [64], P('freq'), may hold values from 0 to 63, each once
- tap_table: float32 [2, 9, 32, 64], replicated, may hold values from -2 to 2
- vel_index: int32 [4, 64, 256], P('depth'), may hold values from 0 to 31
Outputs:
- migrated_image: float32 [4, 64, 256], P('depth')
The draws below stay inside these ranges and needn't reach their ends.
Inputs may be any that keep to these rules, and one draw needn't show every extreme that they name: `freq_slot`: each frequency of the table is named by exactly one slot.
All inputs are finite; a program needn't handle non-finite values.
Results may differ from the reference program's by a relative error of at most 0.00023.
Values sent between devices are 32-bit elements; how exact they have to be, the bound alone decides.
No kernel may reach another device: no remote copies, remote signals or barrier semaphores. Data moves between devices by JAX's collectives and lax.ppermute only.
A program may use at most 64 MiB of HBM per device.

```python
import math
import jax
import jax.numpy as jnp
from jax import lax

NX = 64
NY = 256
TERMS = 9
NV = 32
NF = 64
NZ = 4


def draw_tap_table(key, part):
    key_omega = jax.random.fold_in(key, 11)
    key_slow = jax.random.fold_in(key, 12)
    key_turn = jax.random.fold_in(key, 13)
    omegas = jax.random.uniform(key_omega, (NF, 1), jnp.float32, 5.0, 5.5)
    slowness = jax.random.uniform(key_slow, (1, NV), jnp.float32, 0.9, 1.0)
    turning = jax.random.uniform(key_turn, (NF, NV), jnp.float32, -math.pi, math.pi)
    half_arg = 0.5 * omegas * slowness
    cos_turn = jnp.cos(turning)
    sin_turn = jnp.sin(turning)
    reals = []
    imags = []
    for degree in range(TERMS):
        series = jnp.zeros((NF, NV), jnp.float32)
        for power_no in range(24):
            factor = (-1.0) ** power_no / (math.factorial(power_no) * math.factorial(power_no + degree))
            series = series + factor * half_arg ** (2 * power_no + degree)
        weight_k = 0.97 * (1.0 if degree == 0 else 2.0) * series
        quarter = degree % 4
        unit_real = [1.0, 0.0, -1.0, 0.0][quarter]
        unit_imag = [0.0, 1.0, 0.0, -1.0][quarter]
        base_real = weight_k * unit_real
        base_imag = weight_k * unit_imag
        reals.append(base_real * cos_turn - base_imag * sin_turn)
        imags.append(base_real * sin_turn + base_imag * cos_turn)
    stacked = jnp.stack([jnp.stack(reals, axis=1), jnp.stack(imags, axis=1)], axis=1)
    return jnp.transpose(stacked, (1, 2, 3, 0)).astype(jnp.float32)


def set_ends(drawn, key, low, largest):
    place = [jax.random.randint(jax.random.fold_in(key, axis), (), 0, length) for axis, length in enumerate(drawn.shape)]
    main_axis = drawn.shape.index(max(drawn.shape))
    beside = place[:main_axis] + [(place[main_axis] + 1) % drawn.shape[main_axis]] + place[main_axis + 1:]
    return drawn.at[tuple(place)].set(low).at[tuple(beside)].set(largest)


def shard_levels(stream_key, extent, split, least, high):
    def one(position, shards_of):
        steps = jax.random.uniform(jax.random.fold_in(jax.random.fold_in(stream_key, 6), position), (shards_of,), jnp.float32, least / len(split), high / len(split))
        return jnp.repeat(jnp.exp(steps), extent[position] // shards_of).reshape((-1,) + (1,) * (len(extent) - position - 1))

    loudness = one(*split[0])
    for cut in split[1:]:
        loudness = loudness * one(*cut)
    return loudness


def scatter_about(own_key, dims, scale, reach, split=(), kind=jnp.bfloat16):
    entries = scale * jax.random.normal(own_key, dims, jnp.float32)
    if split:
        entries = entries * shard_levels(own_key, dims, split, -0.22, 0.18)
    return jnp.clip(entries, -reach, reach).astype(kind)


def setup_inputs(seed: int = 0) -> dict:
    splits = jax.random.split(jax.random.key(seed), 5)
    surface = scatter_about(splits[0], (NF, 2, NX, NY), 1.0, 6.0, ((0, 8),), jnp.float32)
    freq_slot = jax.random.permutation(splits[1], NF).astype(jnp.int32)
    tap_table = draw_tap_table(jax.random.fold_in(splits[4], 71), 0)
    vel_index = set_ends(jax.random.randint(splits[3], (NZ, NX, NY), 0, NV), jax.random.fold_in(splits[3], 1), 0, NV - 1).astype(jnp.int32)
    return {"surface": surface, "freq_slot": freq_slot, "tap_table": tap_table, "vel_index": vel_index}


def smooth(wavefield):
    lead = [(0, 0)] * (wavefield.ndim - 2)
    padded = jnp.pad(wavefield, lead + [(1, 1), (1, 1)])
    smoothed = 0.25 * padded[..., :-2, :] + 0.5 * padded[..., 1:-1, :] + 0.25 * padded[..., 2:, :]
    return 0.25 * smoothed[..., :-2] + 0.5 * smoothed[..., 1:-1] + 0.25 * smoothed[..., 2:]

def mcclellan(wavefield):
    return 2.0 * smooth(wavefield) - wavefield

def extrapolate(wavefield, coef_block):
    earlier = wavefield
    current = mcclellan(wavefield)
    real_acc = coef_block[:, 0, 0] * wavefield[:, 0] - coef_block[:, 1, 0] * wavefield[:, 1]
    imag_acc = coef_block[:, 0, 0] * wavefield[:, 1] + coef_block[:, 1, 0] * wavefield[:, 0]
    for degree in range(1, coef_block.shape[2]):
        if degree > 1:
            earlier, current = (current, 2.0 * mcclellan(current) - earlier)
        real_acc = real_acc + coef_block[:, 0, degree] * current[:, 0] - coef_block[:, 1, degree] * current[:, 1]
        imag_acc = imag_acc + coef_block[:, 0, degree] * current[:, 1] + coef_block[:, 1, degree] * current[:, 0]
    return jnp.stack([real_acc, imag_acc], axis=1)

def reference(surface, freq_slot, tap_table, vel_index):
    tap_rows = jnp.moveaxis(jnp.take(tap_table, freq_slot, axis=3), 3, 0)

    def depth_step(wavefield, vel_rows):
        coef_block = jnp.take(tap_rows, vel_rows, axis=3)
        wavefield = extrapolate(wavefield, coef_block)
        return (wavefield, lax.optimization_barrier(jnp.sum(wavefield[:, 0], axis=0)))
    _, stacked = lax.scan(depth_step, surface, vel_index)
    return stacked / math.sqrt(NF)
```

```python
import functools
import math

import jax
import jax.numpy as jnp
from jax import lax
from jax.experimental import pallas as pl
from jax.experimental.pallas import tpu as pltpu
from jax.sharding import PartitionSpec as P

SUB = 8
LANES = 128


def exchange(value, axis, distance):
    count = lax.axis_size(axis)
    return lax.ppermute(value, axis, [(i, i ^ distance) for i in range(count)])


def lane_take(vector, index):
    return jnp.take_along_axis(vector, index, axis=1, mode="promise_in_bounds")


def split_lanes(low, high, index, first_half):
    even = jnp.where(first_half, lane_take(low, index), lane_take(high, index))
    odd = jnp.where(first_half, lane_take(low, index + 1), lane_take(high, index + 1))
    return even, odd


def join_lanes(even, odd, index, is_even):
    low = jnp.where(is_even, lane_take(even, index), lane_take(odd, index))
    high = jnp.where(is_even, lane_take(even, index + LANES // 2), lane_take(odd, index + LANES // 2))
    return low, high


def column(value, rows):
    return [jnp.broadcast_to(value[r : r + 1], (SUB, LANES)) for r in rows]


def image_kernel(
    sizes, scale, slot_ref, surface_ref, tap_ref, *refs
):
    count, local_count, depth_count, levels, terms, entries, vel_count = sizes
    vel_refs = refs[:vel_count]
    keep_ref, send_ref, raw, raw_sem, halves, halves_i, index_ref, table, state, basis = refs[vel_count:]
    depth_pos = lax.axis_index("depth")
    members = [jnp.minimum(depth_pos * count + j, local_count - 1) for j in range(count)]
    copies = [
        pltpu.make_async_copy(surface_ref.at[members[j]], raw.at[j], raw_sem.at[j]) for j in range(count)
    ]
    for copy in copies:
        copy.start()

    lane = lax.broadcasted_iota(jnp.int32, (SUB, LANES), 1)
    row = lax.broadcasted_iota(jnp.int32, (SUB, LANES), 0)
    half = LANES // 2
    first_half = lane < half
    split_index = jnp.where(first_half, 2 * lane, 2 * lane - LANES)
    is_even = lane % 2 == 0
    join_index = lane // 2
    not_first = (lane > 0).astype(jnp.float32)
    not_last = (lane < LANES - 1).astype(jnp.float32)
    not_top = (row > 0).astype(jnp.float32)
    not_bottom = (row < SUB - 1).astype(jnp.float32)

    table_freqs = tap_ref.shape[1]
    freq_lane = lax.broadcasted_iota(jnp.int32, (SUB, table_freqs), 1)
    freq_row = lax.broadcasted_iota(jnp.int32, (SUB, table_freqs), 0)
    wanted = jnp.zeros((SUB, table_freqs), jnp.int32)
    for j in range(count):
        wanted = jnp.where(freq_row == j, slot_ref[members[j]], wanted)
    picked = lax.dot_general(
        (freq_lane == wanted).astype(jnp.float32),
        tap_ref[...],
        (((1,), (1,)), ((), ())),
        precision=lax.Precision.HIGHEST,
        preferred_element_type=jnp.float32,
    )
    per_vector = LANES // entries
    for j in range(count):
        for c in range(2):
            for k in range(terms):
                place = c * terms + k
                vector = place // per_vector
                whole = picked[:, vector * LANES : (vector + 1) * LANES]
                if whole.shape[1] < LANES:
                    whole = jnp.concatenate(
                        [whole, jnp.zeros((SUB, LANES - whole.shape[1]), jnp.float32)], axis=1
                    )
                turn = (place % per_vector) * entries
                if turn:
                    whole = pltpu.roll(whole, LANES - turn, 1)
                table[j, c, k] = jnp.broadcast_to(whole[j : j + 1], (SUB, LANES))

    slot = 0
    for vel_ref in vel_refs:
        for part in range(vel_ref.shape[0] // levels):
            target = jnp.bitwise_xor(depth_pos, slot)
            for level in range(levels):
                for h in range(2):
                    halves_i[h] = vel_ref[part * levels + level, :, h * LANES : (h + 1) * LANES]
                for x in range(SUB):
                    low, high = [halves_i[h, pl.ds(x, SUB, stride=SUB)] for h in range(2)]
                    even, odd = split_lanes(low, high, split_index, first_half)
                    index_ref[target * levels + level, x, 0] = even
                    index_ref[target * levels + level, x, 1] = odd
            slot += 1

    for j in range(count):
        copies[j].wait()
        valid = depth_pos * count + j < local_count
        for c in range(2):
            for h in range(2):
                halves[h] = raw[j, c, :, h * LANES : (h + 1) * LANES]
            for x in range(SUB):
                low, high = [halves[h, pl.ds(x, SUB, stride=SUB)] for h in range(2)]
                even, odd = split_lanes(low, high, split_index, first_half)
                state[j, c, x, 0] = jnp.where(valid, even, 0.0)
                state[j, c, x, 1] = jnp.where(valid, odd, 0.0)

    def spread(value):
        summed = []
        for p in range(2):
            u = [value[x][p] for x in range(SUB)]
            before = pltpu.roll(u[SUB - 1], 1, 0) * not_top
            after = pltpu.roll(u[0], SUB - 1, 0) * not_bottom
            line = [before] + u + [after]
            pairs = [line[i] + line[i + 1] for i in range(SUB + 1)]
            summed.append([pairs[i] + pairs[i + 1] for i in range(SUB)])
        out = []
        for x in range(SUB):
            even, odd = summed[0][x], summed[1][x]
            both = even + odd
            out.append(
                (
                    both + (even + pltpu.roll(odd, 1, 1) * not_first),
                    both + (odd + pltpu.roll(even, LANES - 1, 1) * not_last),
                )
            )
        return out

    def depth_step(z, carry):
        for j in range(count):
            for c in range(2):
                current = [[state[j, c, x, p] for p in range(2)] for x in range(SUB)]
                sums = None
                for k in range(1, terms):
                    wide = spread(current)
                    if k == 1:
                        sums = [[0.125 * wide[x][p] for p in range(2)] for x in range(SUB)]
                    else:
                        sums = [[0.25 * wide[x][p] - sums[x][p] for p in range(2)] for x in range(SUB)]
                    current = [[sums[x][p] - current[x][p] for p in range(2)] for x in range(SUB)]
                    for x in range(SUB):
                        for p in range(2):
                            basis[j, c, k - 1, x, p] = current[x][p]
        for x in range(SUB):
            layers = []
            for p in range(2):
                index = index_ref[z, x, p]
                layer = None
                for j in range(count):
                    real = imag = None
                    for k in range(terms):
                        coef_r = lane_take(table[j, 0, k], index)
                        coef_i = lane_take(table[j, 1, k], index)
                        if k == 0:
                            field_r, field_i = state[j, 0, x, p], state[j, 1, x, p]
                            real = coef_r * field_r - coef_i * field_i
                            imag = coef_r * field_i + coef_i * field_r
                        else:
                            field_r, field_i = basis[j, 0, k - 1, x, p], basis[j, 1, k - 1, x, p]
                            real = real + coef_r * field_r - coef_i * field_i
                            imag = imag + coef_r * field_i + coef_i * field_r
                    state[j, 0, x, p] = real
                    state[j, 1, x, p] = imag
                    layer = real if layer is None else layer + real
                layers.append(layer * scale)
            low, high = join_lanes(layers[0], layers[1], join_index, is_even)
            halves[0, pl.ds(x, SUB, stride=SUB)] = low
            halves[1, pl.ds(x, SUB, stride=SUB)] = high
        place = jnp.bitwise_xor(z // levels, depth_pos)
        level = z % levels

        def put(ref):
            at = (place // 2) * levels + level
            for h in range(2):
                ref[at, :, h * LANES : (h + 1) * LANES] = halves[h]

        pl.when(place % 2 == 0)(functools.partial(put, keep_ref))
        pl.when(place % 2 == 1)(functools.partial(put, send_ref))
        return carry

    lax.fori_loop(0, depth_count * levels, depth_step, 0)


def per_device(surface, freq_slot, tap_table, vel_index):
    local_count, _, rows, columns = surface.shape
    depth_count = lax.axis_size("depth")
    freq_count = lax.axis_size("freq")
    levels = vel_index.shape[0]
    _, terms, entries, table_freqs = tap_table.shape
    count = -(-local_count // depth_count)

    vel_parts = vel_index
    distance = 1
    order = []
    while distance < depth_count:
        order.append(distance)
        distance *= 2
    vel_parts = vel_index
    for distance in order:
        vel_parts = jnp.concatenate([vel_parts, exchange(vel_parts, "depth", distance)], axis=0)
    vels = [vel_parts]

    scale = 1.0 / math.sqrt(local_count * freq_count)
    sizes = (count, local_count, depth_count, levels, terms, entries, len(vels))
    half = jax.ShapeDtypeStruct((depth_count // 2 * levels, rows, columns), jnp.float32)
    vmem = pl.BlockSpec(memory_space=pltpu.VMEM)
    keep, send = pl.pallas_call(
        functools.partial(image_kernel, sizes, scale),
        out_shape=(half, half),
        in_specs=[
            pl.BlockSpec(memory_space=pltpu.SMEM),
            pl.BlockSpec(memory_space=pl.ANY),
            vmem,
        ]
        + [vmem] * len(vels),
        out_specs=(vmem, vmem),
        scratch_shapes=[
            pltpu.VMEM((count, 2, rows, columns), jnp.float32),
            pltpu.SemaphoreType.DMA((count,)),
            pltpu.VMEM((2, rows, LANES), jnp.float32),
            pltpu.VMEM((2, rows, LANES), jnp.int32),
            pltpu.VMEM((depth_count * levels, SUB, 2, SUB, LANES), jnp.int32),
            pltpu.VMEM((count, 2, terms, SUB, LANES), jnp.float32),
            pltpu.VMEM((count, 2, SUB, 2, SUB, LANES), jnp.float32),
            pltpu.VMEM((count, 2, terms - 1, SUB, 2, SUB, LANES), jnp.float32),
        ],
        compiler_params=pltpu.CompilerParams(vmem_limit_bytes=32 * 1024 * 1024),
    )(freq_slot, surface, tap_table.reshape(2 * terms * entries, table_freqs), *vels)

    image = keep + exchange(send, "depth", 1)
    distance = 2
    while distance < depth_count:
        image = image.reshape((-1, 2, levels, rows, columns))
        image = (image[:, 0] + exchange(image[:, 1], "depth", distance)).reshape((-1, rows, columns))
        distance *= 2
    distance = 1
    while distance < freq_count:
        image = image + exchange(image, "freq", distance)
        distance *= 2
    return image


def solution(mesh):
    in_specs = (P("freq", None, None, None), P("freq"), P(), P("depth", None, None))
    out_specs = P("depth", None, None)
    return jax.shard_map(
        per_device, mesh=mesh, in_specs=in_specs, out_specs=out_specs, check_vma=False
    )
```

```python
import functools
import math

import jax
import jax.numpy as jnp
from jax import lax
from jax.experimental import pallas as pl
from jax.experimental.pallas import tpu as pltpu
from jax.sharding import PartitionSpec as P

SUB = 8
LANES = 128
PAIR = 2
QUAD = 4
ENTRY_SPAN = LANES // PAIR


def exchange(value, axis, flip):
    count = lax.axis_size(axis)
    return lax.ppermute(value, axis, [(i, i ^ flip) for i in range(count)])


def lane_take(vector, index):
    return jnp.take_along_axis(vector, index, axis=1, mode="promise_in_bounds")


def lane_number():
    return lax.broadcasted_iota(jnp.int32, (SUB, LANES), 1)


def edge_masks():
    lane = lane_number() % ENTRY_SPAN
    row = lax.broadcasted_iota(jnp.int32, (SUB, LANES), 0)
    return (
        (lane > 0).astype(jnp.float32),
        (lane < ENTRY_SPAN - 1).astype(jnp.float32),
        (row > 0).astype(jnp.float32),
        (row < SUB - 1).astype(jnp.float32),
    )


def chebyshev(start, terms, masks, put):
    left_mask, right_mask, top_mask, bottom_mask = masks
    current, sums = start, None
    for k in range(1, terms):
        lines = []
        for y in range(QUAD):
            column = [current[x][y] for x in range(SUB)]
            above = pltpu.roll(column[SUB - 1], 1, 0) * top_mask
            below = pltpu.roll(column[0], SUB - 1, 0) * bottom_mask
            lines.append([above] + column + [below])
        pairs = [lines[y][0] + lines[y][1] for y in range(QUAD)]
        following, following_sums = [], []
        for x in range(SUB):
            later = [lines[y][x + 1] + lines[y][x + 2] for y in range(QUAD)]
            line = [pairs[y] + later[y] for y in range(QUAD)]
            pairs = later
            left = pltpu.roll(line[QUAD - 1], 1, 1) * left_mask
            right = pltpu.roll(line[0], LANES - 1, 1) * right_mask
            line = [left] + line + [right]
            sides = [line[i] + line[i + 1] for i in range(QUAD + 1)]
            new, new_sums = [], []
            for y in range(QUAD):
                wide = sides[y] + sides[y + 1]
                total = 0.125 * wide if k == 1 else 0.25 * wide - sums[x][y]
                value = total - current[x][y]
                put(k, x, y, value)
                new.append(value)
                new_sums.append(total)
            following.append(new)
            following_sums.append(new_sums)
        current, sums = following, following_sums


def split_index(y):
    return (lane_number() % (LANES // QUAD)) * QUAD + y


def first_kernel(sizes, slot_ref, surface_ref, tap_ref, table_ref, basis_ref, raw, raw_sem, halves):
    groups, count, local_count, terms, entries = sizes
    first = lax.axis_index("depth") * count
    members = [jnp.minimum(first + j, local_count - 1) for j in range(count)]
    copies = [pltpu.make_async_copy(surface_ref.at[members[j]], raw.at[j], raw_sem.at[j]) for j in range(count)]
    for copy in copies:
        copy.start()

    table_freqs = tap_ref.shape[1]
    rows = -(-count // SUB) * SUB
    freq_lane = lax.broadcasted_iota(jnp.int32, (rows, table_freqs), 1)
    freq_row = lax.broadcasted_iota(jnp.int32, (rows, table_freqs), 0)
    wanted = jnp.zeros((rows, table_freqs), jnp.int32)
    for j in range(count):
        wanted = jnp.where(freq_row == j, slot_ref[members[j]], wanted)
    picked = lax.dot_general(
        (freq_lane == wanted).astype(jnp.float32),
        tap_ref[...],
        (((1,), (1,)), ((), ())),
        precision=lax.Precision.HIGHEST,
        preferred_element_type=jnp.float32,
    )
    lane = lane_number()
    per_vector = LANES // entries
    for g in range(groups):
        for c in range(2):
            for k in range(terms):
                place = c * terms + k
                vector = place // per_vector
                whole = picked[:, vector * LANES : (vector + 1) * LANES]
                if whole.shape[1] < LANES:
                    whole = jnp.concatenate([whole, jnp.zeros((rows, LANES - whole.shape[1]), jnp.float32)], axis=1)
                sides = []
                for i in range(PAIR):
                    turn = ((place % per_vector) * entries - i * ENTRY_SPAN) % LANES
                    turned = pltpu.roll(whole, LANES - turn, 1) if turn else whole
                    j = min(g * PAIR + i, count - 1)
                    sides.append(jnp.broadcast_to(turned[j : j + 1], (SUB, LANES)))
                table_ref[g, c, k] = jnp.where(lane < ENTRY_SPAN, sides[0], sides[1])

    for copy in copies:
        copy.wait()
    masks = edge_masks()
    in_low = lane % ENTRY_SPAN < ENTRY_SPAN // 2
    for g in range(groups):
        for c in range(2):
            for i in range(PAIR):
                j = min(g * PAIR + i, count - 1)
                for h in range(2):
                    halves[i, h] = raw[j, c, :, h * LANES : (h + 1) * LANES]
            start = []
            for x in range(SUB):
                line = []
                for y in range(QUAD):
                    index = split_index(y)
                    sides = []
                    for i in range(PAIR):
                        low, high = [lane_take(halves[i, h, pl.ds(x, SUB, stride=SUB)], index) for h in range(2)]
                        side = jnp.where(in_low, low, high)
                        j = g * PAIR + i
                        if j >= count:
                            side = jnp.zeros_like(side)
                        elif count * lax.axis_size("depth") > local_count:
                            side = jnp.where(first + j < local_count, side, 0.0)
                        sides.append(side)
                    value = jnp.where(lane < ENTRY_SPAN, sides[0], sides[1])
                    basis_ref[g, 0, c, x, y] = value
                    line.append(value)
                start.append(line)

            def put(k, x, y, value):
                basis_ref[g, k, c, x, y] = value

            chebyshev(start, terms, masks, put)


def image_kernel(sizes, scale, table_ref, first_ref, *refs):
    groups, depth_count, levels, terms = sizes
    vel_refs = refs[:depth_count]
    keep_ref, send_ref, halves, halves_i, index_ref, basis = refs[depth_count:]
    depth_pos = lax.axis_index("depth")
    depths = depth_count * levels
    lane = lane_number()
    in_low = lane % ENTRY_SPAN < ENTRY_SPAN // 2
    masks = edge_masks()

    table_base = jnp.where(lane < ENTRY_SPAN, 0, ENTRY_SPAN)
    for slot, vel_ref in enumerate(vel_refs):
        target = jnp.bitwise_xor(depth_pos, slot) * levels
        for level in range(levels):
            for h in range(2):
                halves_i[h] = vel_ref[level, :, h * LANES : (h + 1) * LANES]
            for x in range(SUB):
                low, high = [halves_i[h, pl.ds(x, SUB, stride=SUB)] for h in range(2)]
                for y in range(QUAD):
                    index = split_index(y)
                    entry = jnp.where(in_low, lane_take(low, index), lane_take(high, index))
                    index_ref[target + level, x, y] = entry + table_base

    low_index = lane // QUAD
    quarter = lane % QUAD

    def accumulate(z, source):
        for x in range(SUB):
            layers = []
            for y in range(QUAD):
                index = index_ref[z, x, y]
                layer = None
                for g in range(groups):
                    real = imag = None
                    for k in range(terms):
                        coef_r = lane_take(table_ref[g, 0, k], index)
                        coef_i = lane_take(table_ref[g, 1, k], index)
                        field_r, field_i = source[g, k, 0, x, y], source[g, k, 1, x, y]
                        if k == 0:
                            real = coef_r * field_r - coef_i * field_i
                            imag = coef_r * field_i + coef_i * field_r
                        else:
                            real = real + coef_r * field_r - coef_i * field_i
                            imag = imag + coef_r * field_i + coef_i * field_r
                    basis[g, 0, 0, x, y] = real
                    basis[g, 0, 1, x, y] = imag
                    layer = real if layer is None else layer + real
                layers.append((layer + pltpu.roll(layer, ENTRY_SPAN, 1)) * scale)
            for h in range(2):
                index = low_index + h * (LANES // QUAD)
                whole = lane_take(layers[0], index)
                for y in range(1, QUAD):
                    whole = jnp.where(quarter == y, lane_take(layers[y], index), whole)
                halves[h, pl.ds(x, SUB, stride=SUB)] = whole
        place = jnp.bitwise_xor(z // levels, depth_pos)
        level = z % levels

        def emit(ref):
            at = (place // 2) * levels + level
            for h in range(2):
                ref[at, :, h * LANES : (h + 1) * LANES] = halves[h]

        pl.when(place % 2 == 0)(functools.partial(emit, keep_ref))
        pl.when(place % 2 == 1)(functools.partial(emit, send_ref))

    accumulate(0, first_ref)

    def depth_step(z, carry):
        for g in range(groups):
            for c in range(2):
                start = [[basis[g, 0, c, x, y] for y in range(QUAD)] for x in range(SUB)]

                def put(k, x, y, value):
                    basis[g, k, c, x, y] = value

                chebyshev(start, terms, masks, put)
        accumulate(z, basis)
        return carry

    lax.fori_loop(1, depths, depth_step, 0)


def per_device(surface, freq_slot, tap_table, vel_index):
    local_count, _, rows, columns = surface.shape
    depth_count = lax.axis_size("depth")
    freq_count = lax.axis_size("freq")
    levels = vel_index.shape[0]
    _, terms, entries, table_freqs = tap_table.shape
    count = -(-local_count // depth_count)
    groups = -(-count // PAIR)
    depths = depth_count * levels
    vmem = pl.BlockSpec(memory_space=pltpu.VMEM)
    params = pltpu.CompilerParams(vmem_limit_bytes=40 * 1024 * 1024)

    vels = [vel_index] + [exchange(vel_index, "depth", flip) for flip in range(1, depth_count)]

    basis_shape = (groups, terms, 2, SUB, QUAD, SUB, LANES)
    table, basis = pl.pallas_call(
        functools.partial(first_kernel, (groups, count, local_count, terms, entries)),
        out_shape=(
            jax.ShapeDtypeStruct((groups, 2, terms, SUB, LANES), jnp.float32),
            jax.ShapeDtypeStruct(basis_shape, jnp.float32),
        ),
        in_specs=[
            pl.BlockSpec(memory_space=pltpu.SMEM),
            pl.BlockSpec(memory_space=pl.ANY),
            vmem,
        ],
        out_specs=(vmem, vmem),
        scratch_shapes=[
            pltpu.VMEM((count, 2, rows, columns), jnp.float32),
            pltpu.SemaphoreType.DMA((count,)),
            pltpu.VMEM((PAIR, 2, rows, LANES), jnp.float32),
        ],
        compiler_params=params,
        cost_estimate=pl.CostEstimate(flops=200_000_000, bytes_accessed=16_000_000, transcendentals=0),
    )(freq_slot, surface, tap_table.reshape(2 * terms * entries, table_freqs))

    scale = 1.0 / math.sqrt(local_count * freq_count)
    half = jax.ShapeDtypeStruct((depths // 2, rows, columns), jnp.float32)
    keep, send = pl.pallas_call(
        functools.partial(image_kernel, (groups, depth_count, levels, terms), scale),
        out_shape=(half, half),
        in_specs=[vmem] * (2 + depth_count),
        out_specs=(vmem, vmem),
        scratch_shapes=[
            pltpu.VMEM((2, rows, LANES), jnp.float32),
            pltpu.VMEM((2, rows, LANES), jnp.int32),
            pltpu.VMEM((depths, SUB, QUAD, SUB, LANES), jnp.int32),
            pltpu.VMEM(basis_shape, jnp.float32),
        ],
        compiler_params=params,
    )(table, basis, *vels)

    image = keep + exchange(send, "depth", 1)
    distance = 2
    while distance < depth_count:
        image = image.reshape((-1, 2, levels, rows, columns))
        image = (image[:, 0] + exchange(image[:, 1], "depth", distance)).reshape((-1, rows, columns))
        distance *= 2
    distance = 1
    while distance < freq_count:
        if distance == 1 and freq_count >= 4:
            image = image + exchange(image, "freq", 1) + (exchange(image, "freq", 2) + exchange(image, "freq", 3))
            distance = 4
        else:
            image = image + exchange(image, "freq", distance)
            distance *= 2
    return image


def solution(mesh):
    in_specs = (P("freq", None, None, None), P("freq"), P(), P("depth", None, None))
    out_specs = P("depth", None, None)
    return jax.shard_map(
        per_device, mesh=mesh, in_specs=in_specs, out_specs=out_specs, check_vma=False
    )
```

```python
import functools
import math

import jax
import jax.numpy as jnp
from jax import lax
from jax.experimental import pallas as pl
from jax.experimental.pallas import tpu as pltpu
from jax.sharding import PartitionSpec as P

SUB = 8
LANES = 128
PAIR = 2
QUAD = 4
ENTRY_SPAN = LANES // PAIR


def exchange(value, axis, flip):
    count = lax.axis_size(axis)
    return lax.ppermute(value, axis, [(i, i ^ flip) for i in range(count)])


def lane_take(vector, index):
    return jnp.take_along_axis(vector, index, axis=1, mode="promise_in_bounds")


def lane_number():
    return lax.broadcasted_iota(jnp.int32, (SUB, LANES), 1)


def edge_masks():
    lane = lane_number() % ENTRY_SPAN
    row = lax.broadcasted_iota(jnp.int32, (SUB, LANES), 0)
    return (
        (lane > 0).astype(jnp.float32),
        (lane < ENTRY_SPAN - 1).astype(jnp.float32),
        (row > 0).astype(jnp.float32),
        (row < SUB - 1).astype(jnp.float32),
    )


def chebyshev(start, terms, masks, put):
    left_mask, right_mask, top_mask, bottom_mask = masks
    current, sums = start, None
    for k in range(1, terms):
        lines = []
        for y in range(QUAD):
            column = [current[x][y] for x in range(SUB)]
            above = pltpu.roll(column[SUB - 1], 1, 0) * top_mask
            below = pltpu.roll(column[0], SUB - 1, 0) * bottom_mask
            lines.append([above] + column + [below])
        pairs = [lines[y][0] + lines[y][1] for y in range(QUAD)]
        following, following_sums = [], []
        for x in range(SUB):
            later = [lines[y][x + 1] + lines[y][x + 2] for y in range(QUAD)]
            line = [pairs[y] + later[y] for y in range(QUAD)]
            pairs = later
            left = pltpu.roll(line[QUAD - 1], 1, 1) * left_mask
            right = pltpu.roll(line[0], LANES - 1, 1) * right_mask
            line = [left] + line + [right]
            sides = [line[i] + line[i + 1] for i in range(QUAD + 1)]
            new, new_sums = [], []
            for y in range(QUAD):
                wide = sides[y] + sides[y + 1]
                total = 0.125 * wide if k == 1 else 0.25 * wide - sums[x][y]
                value = total - current[x][y]
                put(k, x, y, value)
                new.append(value)
                new_sums.append(total)
            following.append(new)
            following_sums.append(new_sums)
        current, sums = following, following_sums


def split_index(y):
    return (lane_number() % (LANES // QUAD)) * QUAD + y


def first_kernel(
    sizes, slot_hbm, surface_ref, tap_hbm, vel_hbm, table_ref, basis_ref, vel_ref, raw, raw_sem, halves, slot_ref, tap_ref, sems
):
    groups, count, local_count, terms, entries = sizes
    first = lax.axis_index("depth") * count
    members = [jnp.minimum(first + j, local_count - 1) for j in range(count)]
    slot_copy = pltpu.make_async_copy(slot_hbm, slot_ref, sems.at[0])
    tap_copy = pltpu.make_async_copy(tap_hbm, tap_ref, sems.at[1])
    vel_copy = pltpu.make_async_copy(vel_hbm, vel_ref, sems.at[2])
    copies = [pltpu.make_async_copy(surface_ref.at[members[j]], raw.at[j], raw_sem.at[j]) for j in range(count)]
    slot_copy.start()
    tap_copy.start()
    for copy in copies:
        copy.start()
    vel_copy.start()
    slot_copy.wait()
    tap_copy.wait()

    table_freqs = tap_ref.shape[1]
    rows = -(-count // SUB) * SUB
    freq_lane = lax.broadcasted_iota(jnp.int32, (rows, table_freqs), 1)
    freq_row = lax.broadcasted_iota(jnp.int32, (rows, table_freqs), 0)
    wanted = jnp.zeros((rows, table_freqs), jnp.int32)
    for j in range(count):
        wanted = jnp.where(freq_row == j, slot_ref[members[j]], wanted)
    picked = lax.dot_general(
        (freq_lane == wanted).astype(jnp.float32),
        tap_ref[...],
        (((1,), (1,)), ((), ())),
        precision=lax.Precision.HIGHEST,
        preferred_element_type=jnp.float32,
    )
    lane = lane_number()
    per_vector = LANES // entries
    for g in range(groups):
        for c in range(2):
            for k in range(terms):
                place = c * terms + k
                vector = place // per_vector
                whole = picked[:, vector * LANES : (vector + 1) * LANES]
                if whole.shape[1] < LANES:
                    whole = jnp.concatenate([whole, jnp.zeros((rows, LANES - whole.shape[1]), jnp.float32)], axis=1)
                sides = []
                for i in range(PAIR):
                    turn = ((place % per_vector) * entries - i * ENTRY_SPAN) % LANES
                    turned = pltpu.roll(whole, LANES - turn, 1) if turn else whole
                    j = min(g * PAIR + i, count - 1)
                    sides.append(jnp.broadcast_to(turned[j : j + 1], (SUB, LANES)))
                table_ref[g, c, k] = jnp.where(lane < ENTRY_SPAN, sides[0], sides[1])

    for copy in copies:
        copy.wait()
    masks = edge_masks()
    in_low = lane % ENTRY_SPAN < ENTRY_SPAN // 2
    for g in range(groups):
        for c in range(2):
            for i in range(PAIR):
                j = min(g * PAIR + i, count - 1)
                for h in range(2):
                    halves[g, c, i, h] = raw[j, c, :, h * LANES : (h + 1) * LANES]
    for y in range(QUAD):
        index = split_index(y)
        for g in range(groups):
            for c in range(2):
                for x in range(SUB):
                    sides = []
                    for i in range(PAIR):
                        low, high = [lane_take(halves[g, c, i, h, pl.ds(x, SUB, stride=SUB)], index) for h in range(2)]
                        side = jnp.where(in_low, low, high)
                        j = g * PAIR + i
                        if j >= count:
                            side = jnp.zeros_like(side)
                        elif count * lax.axis_size("depth") > local_count:
                            side = jnp.where(first + j < local_count, side, 0.0)
                        sides.append(side)
                    basis_ref[g, 0, c, x, y] = jnp.where(lane < ENTRY_SPAN, sides[0], sides[1])
    for g in range(groups):
        for c in range(2):
            start = [[basis_ref[g, 0, c, x, y] for y in range(QUAD)] for x in range(SUB)]

            def put(k, x, y, value):
                basis_ref[g, k, c, x, y] = value

            chebyshev(start, terms, masks, put)
    vel_copy.wait()


def image_kernel(sizes, scale, table_ref, first_ref, *refs):
    groups, depth_count, levels, terms = sizes
    vel_refs = refs[:depth_count]
    keep_ref, send_ref, numbers, halves, index_ref, layers, basis = refs[depth_count:]
    depth_pos = lax.axis_index("depth")
    depths = depth_count * levels
    columns = QUAD * ENTRY_SPAN
    masks = edge_masks()

    source = lax.broadcasted_iota(jnp.int32, (columns, QUAD * LANES), 0)
    place = lax.broadcasted_iota(jnp.int32, (columns, QUAD * LANES), 1)
    split = (source == (place % ENTRY_SPAN) * QUAD + place // LANES).astype(jnp.float32).astype(jnp.bfloat16)

    table_base = jnp.where(lane_number() < ENTRY_SPAN, 0, ENTRY_SPAN)
    for slot, vel_ref in enumerate(vel_refs):
        target = jnp.bitwise_xor(depth_pos, slot) * levels
        for level in range(levels):
            spread = jnp.dot(
                vel_ref[level].astype(jnp.float32).astype(jnp.bfloat16), split, preferred_element_type=jnp.float32
            ).astype(jnp.int32)
            for y in range(QUAD):
                numbers[y] = spread[:, y * LANES : (y + 1) * LANES]
            for x in range(SUB):
                for y in range(QUAD):
                    index_ref[target + level, x, y] = numbers[y, pl.ds(x, SUB, stride=SUB)] + table_base

    def first_terms(k, carry):
        for g in range(groups):
            for c in range(2):
                basis[g, k, c] = first_ref[g, k, c]
        return carry

    lax.fori_loop(0, terms, first_terms, 0)

    def depth_step(z, carry):
        for x in range(SUB):
            for y in range(QUAD):
                index = index_ref[z, x, y]
                layer = None
                for g in range(groups):
                    real = imag = None
                    for k in range(terms):
                        coef_r = lane_take(table_ref[g, 0, k], index)
                        coef_i = lane_take(table_ref[g, 1, k], index)
                        field_r, field_i = basis[g, k, 0, x, y], basis[g, k, 1, x, y]
                        if k == 0:
                            real = coef_r * field_r - coef_i * field_i
                            imag = coef_r * field_i + coef_i * field_r
                        else:
                            real = real + coef_r * field_r - coef_i * field_i
                            imag = imag + coef_r * field_i + coef_i * field_r
                    basis[g, 0, 0, x, y] = real
                    basis[g, 0, 1, x, y] = imag
                    layer = real if layer is None else layer + real
                layers[z, y, x * SUB : (x + 1) * SUB] = layer * scale

        @pl.when(z < depths - 1)
        def _():
            for g in range(groups):
                for c in range(2):
                    start = [[basis[g, 0, c, x, y] for y in range(QUAD)] for x in range(SUB)]

                    def put(k, x, y, value):
                        basis[g, k, c, x, y] = value

                    chebyshev(start, terms, masks, put)

        return carry

    lax.fori_loop(0, depths, depth_step, 0)

    turned = lax.broadcasted_iota(jnp.int32, (LANES, columns), 0) % ENTRY_SPAN * QUAD
    wanted = lax.broadcasted_iota(jnp.int32, (LANES, columns), 1)
    joins = [(wanted == turned + y).astype(jnp.float32).astype(jnp.bfloat16) for y in range(QUAD)]

    def join(z, carry):
        whole = None
        for y in range(QUAD):
            rest = layers[z, y]
            for part in range(3):
                piece = rest.astype(jnp.bfloat16)
                rest = rest - piece.astype(jnp.float32)
                product = jnp.dot(piece, joins[y], preferred_element_type=jnp.float32)
                whole = product if whole is None else whole + product
        for h in range(2):
            for x in range(SUB):
                halves[h, pl.ds(x, SUB, stride=SUB)] = whole[x * SUB : (x + 1) * SUB, h * LANES : (h + 1) * LANES]
        place = jnp.bitwise_xor(z // levels, depth_pos)
        level = z % levels

        def emit(ref):
            at = (place // 2) * levels + level
            for h in range(2):
                ref[at, :, h * LANES : (h + 1) * LANES] = halves[h]

        pl.when(place % 2 == 0)(functools.partial(emit, keep_ref))
        pl.when(place % 2 == 1)(functools.partial(emit, send_ref))
        return carry

    lax.fori_loop(0, depths, join, 0)


def per_device(surface, freq_slot, tap_table, vel_index):
    local_count, _, rows, columns = surface.shape
    depth_count = lax.axis_size("depth")
    freq_count = lax.axis_size("freq")
    levels = vel_index.shape[0]
    _, terms, entries, table_freqs = tap_table.shape
    count = -(-local_count // depth_count)
    groups = -(-count // PAIR)
    depths = depth_count * levels
    vmem = pl.BlockSpec(memory_space=pltpu.VMEM)
    params = pltpu.CompilerParams(vmem_limit_bytes=40 * 1024 * 1024)

    vels = [exchange(vel_index, "depth", flip) for flip in range(1, depth_count)]

    basis_shape = (groups, terms, 2, SUB, QUAD, SUB, LANES)
    hbm = pl.BlockSpec(memory_space=pltpu.HBM)
    table, basis, own_vel = pl.pallas_call(
        functools.partial(first_kernel, (groups, count, local_count, terms, entries)),
        out_shape=(
            jax.ShapeDtypeStruct((groups, 2, terms, SUB, LANES), jnp.float32),
            jax.ShapeDtypeStruct(basis_shape, jnp.float32),
            jax.ShapeDtypeStruct(vel_index.shape, jnp.int32),
        ),
        in_specs=[hbm] * 4,
        out_specs=(vmem, vmem, vmem),
        scratch_shapes=[
            pltpu.VMEM((count, 2, rows, columns), jnp.float32),
            pltpu.SemaphoreType.DMA((count,)),
            pltpu.VMEM((groups, 2, PAIR, 2, rows, LANES), jnp.float32),
            pltpu.SMEM((local_count,), jnp.int32),
            pltpu.VMEM((2 * terms * entries, table_freqs), jnp.float32),
            pltpu.SemaphoreType.DMA((3,)),
        ],
        compiler_params=params,
        cost_estimate=pl.CostEstimate(flops=200_000_000, bytes_accessed=16_000_000, transcendentals=0),
    )(freq_slot, surface, tap_table.reshape(2 * terms * entries, table_freqs), vel_index)

    scale = 1.0 / math.sqrt(local_count * freq_count)
    half = jax.ShapeDtypeStruct((depths // 2, rows, columns), jnp.float32)
    keep, send = pl.pallas_call(
        functools.partial(image_kernel, (groups, depth_count, levels, terms), scale),
        out_shape=(half, half),
        in_specs=[vmem] * (2 + depth_count),
        out_specs=(vmem, vmem),
        scratch_shapes=[
            pltpu.VMEM((QUAD, rows, LANES), jnp.int32),
            pltpu.VMEM((2, rows, LANES), jnp.float32),
            pltpu.VMEM((depths, SUB, QUAD, SUB, LANES), jnp.int32),
            pltpu.VMEM((depths, QUAD, rows, LANES), jnp.float32),
            pltpu.VMEM(basis_shape, jnp.float32),
        ],
        compiler_params=params,
    )(table, basis, own_vel, *vels)

    image = keep + exchange(send, "depth", 1)
    distance = 2
    while distance < depth_count:
        image = image.reshape((-1, 2, levels, rows, columns))
        image = (image[:, 0] + exchange(image[:, 1], "depth", distance)).reshape((-1, rows, columns))
        distance *= 2
    distance = 1
    while distance < freq_count:
        if distance == 1 and freq_count >= 4:
            image = image + exchange(image, "freq", 1) + (exchange(image, "freq", 2) + exchange(image, "freq", 3))
            distance = 4
        else:
            image = image + exchange(image, "freq", distance)
            distance *= 2
    return image


def solution(mesh):
    in_specs = (P("freq", None, None, None), P("freq"), P(), P("depth", None, None))
    out_specs = P("depth", None, None)
    return jax.shard_map(
        per_device, mesh=mesh, in_specs=in_specs, out_specs=out_specs, check_vma=False
    )
```

```python
import functools
import math

import jax
import jax.numpy as jnp
from jax import lax
from jax.experimental import pallas as pl
from jax.experimental.pallas import tpu as pltpu
from jax.sharding import PartitionSpec as P

SUB = 8
LANES = 128
PAIR = 2
QUAD = 4
ENTRY_SPAN = LANES // PAIR


def exchange(value, axis, flip):
    count = lax.axis_size(axis)
    return lax.ppermute(value, axis, [(i, i ^ flip) for i in range(count)])


def lane_take(vector, index):
    return jnp.take_along_axis(vector, index, axis=1, mode="promise_in_bounds")


def lane_number():
    return lax.broadcasted_iota(jnp.int32, (SUB, LANES), 1)


def edge_masks():
    lane = lane_number() % ENTRY_SPAN
    row = lax.broadcasted_iota(jnp.int32, (SUB, LANES), 0)
    return (
        (lane > 0).astype(jnp.float32),
        (lane < ENTRY_SPAN - 1).astype(jnp.float32),
        (row > 0).astype(jnp.float32),
        (row < SUB - 1).astype(jnp.float32),
    )


def chebyshev(start, terms, masks, put):
    left_mask, right_mask, top_mask, bottom_mask = masks
    current, sums = start, None
    for k in range(1, terms):
        lines = []
        for y in range(QUAD):
            column = [current[x][y] for x in range(SUB)]
            above = pltpu.roll(column[SUB - 1], 1, 0) * top_mask
            below = pltpu.roll(column[0], SUB - 1, 0) * bottom_mask
            lines.append([above] + column + [below])
        pairs = [lines[y][0] + lines[y][1] for y in range(QUAD)]
        following, following_sums = [], []
        for x in range(SUB):
            later = [lines[y][x + 1] + lines[y][x + 2] for y in range(QUAD)]
            line = [pairs[y] + later[y] for y in range(QUAD)]
            pairs = later
            left = pltpu.roll(line[QUAD - 1], 1, 1) * left_mask
            right = pltpu.roll(line[0], LANES - 1, 1) * right_mask
            line = [left] + line + [right]
            sides = [line[i] + line[i + 1] for i in range(QUAD + 1)]
            new, new_sums = [], []
            for y in range(QUAD):
                wide = sides[y] + sides[y + 1]
                total = 0.125 * wide if k == 1 else 0.25 * wide - sums[x][y]
                value = total - current[x][y]
                put(k, x, y, value)
                new.append(value)
                new_sums.append(total)
            following.append(new)
            following_sums.append(new_sums)
        current, sums = following, following_sums


def split_index(y):
    return (lane_number() % (LANES // QUAD)) * QUAD + y


def first_kernel(
    sizes, slot_hbm, surface_ref, tap_hbm, vel_hbm, table_ref, basis_ref, vel_ref, raw, raw_sem, halves, slot_ref, tap_ref, sems
):
    groups, count, local_count, terms, entries = sizes
    first = lax.axis_index("depth") * count
    members = [jnp.minimum(first + j, local_count - 1) for j in range(count)]
    slot_copy = pltpu.make_async_copy(slot_hbm, slot_ref, sems.at[0])
    tap_copy = pltpu.make_async_copy(tap_hbm, tap_ref, sems.at[1])
    vel_copy = pltpu.make_async_copy(vel_hbm, vel_ref, sems.at[2])
    copies = [pltpu.make_async_copy(surface_ref.at[members[j]], raw.at[j], raw_sem.at[j]) for j in range(count)]
    slot_copy.start()
    tap_copy.start()
    for copy in copies:
        copy.start()
    vel_copy.start()
    slot_copy.wait()
    tap_copy.wait()

    table_freqs = tap_ref.shape[1]
    rows = -(-count // SUB) * SUB
    freq_lane = lax.broadcasted_iota(jnp.int32, (rows, table_freqs), 1)
    freq_row = lax.broadcasted_iota(jnp.int32, (rows, table_freqs), 0)
    wanted = jnp.zeros((rows, table_freqs), jnp.int32)
    for j in range(count):
        wanted = jnp.where(freq_row == j, slot_ref[members[j]], wanted)
    picked = lax.dot_general(
        (freq_lane == wanted).astype(jnp.float32),
        tap_ref[...],
        (((1,), (1,)), ((), ())),
        precision=lax.Precision.HIGHEST,
        preferred_element_type=jnp.float32,
    )
    lane = lane_number()
    per_vector = LANES // entries
    for g in range(groups):
        for c in range(2):
            for k in range(terms):
                place = c * terms + k
                vector = place // per_vector
                whole = picked[:, vector * LANES : (vector + 1) * LANES]
                if whole.shape[1] < LANES:
                    whole = jnp.concatenate([whole, jnp.zeros((rows, LANES - whole.shape[1]), jnp.float32)], axis=1)
                sides = []
                for i in range(PAIR):
                    turn = ((place % per_vector) * entries - i * ENTRY_SPAN) % LANES
                    turned = pltpu.roll(whole, LANES - turn, 1) if turn else whole
                    j = min(g * PAIR + i, count - 1)
                    sides.append(jnp.broadcast_to(turned[j : j + 1], (SUB, LANES)))
                table_ref[g, c, k] = jnp.where(lane < ENTRY_SPAN, sides[0], sides[1])

    for copy in copies:
        copy.wait()
    masks = edge_masks()
    in_low = lane % ENTRY_SPAN < ENTRY_SPAN // 2
    for g in range(groups):
        for c in range(2):
            for i in range(PAIR):
                j = min(g * PAIR + i, count - 1)
                for h in range(2):
                    halves[g, c, i, h] = raw[j, c, :, h * LANES : (h + 1) * LANES]
    for y in range(QUAD):
        index = split_index(y)
        for g in range(groups):
            for c in range(2):
                for x in range(SUB):
                    sides = []
                    for i in range(PAIR):
                        low, high = [lane_take(halves[g, c, i, h, pl.ds(x, SUB, stride=SUB)], index) for h in range(2)]
                        side = jnp.where(in_low, low, high)
                        j = g * PAIR + i
                        if j >= count:
                            side = jnp.zeros_like(side)
                        elif count * lax.axis_size("depth") > local_count:
                            side = jnp.where(first + j < local_count, side, 0.0)
                        sides.append(side)
                    basis_ref[g, 0, c, x, y] = jnp.where(lane < ENTRY_SPAN, sides[0], sides[1])
    for g in range(groups):
        for c in range(2):
            start = [[basis_ref[g, 0, c, x, y] for y in range(QUAD)] for x in range(SUB)]

            def put(k, x, y, value):
                basis_ref[g, k, c, x, y] = value

            chebyshev(start, terms, masks, put)
    vel_copy.wait()


def image_kernel(sizes, scale, table_ref, first_ref, *refs):
    groups, depth_count, levels, terms = sizes
    vel_refs = refs[:depth_count]
    keep_ref, send_ref, numbers, index_ref, layers, basis = refs[depth_count:]
    depth_pos = lax.axis_index("depth")
    depths = depth_count * levels
    columns = QUAD * ENTRY_SPAN
    masks = edge_masks()

    source = lax.broadcasted_iota(jnp.int32, (columns, QUAD * LANES), 0)
    place = lax.broadcasted_iota(jnp.int32, (columns, QUAD * LANES), 1)
    split = (source == (place % ENTRY_SPAN) * QUAD + place // LANES).astype(jnp.float32).astype(jnp.bfloat16)

    table_base = jnp.where(lane_number() < ENTRY_SPAN, 0, ENTRY_SPAN)
    for slot, vel_ref in enumerate(vel_refs):
        target = jnp.bitwise_xor(depth_pos, slot) * levels
        for level in range(levels):
            spread = jnp.dot(
                vel_ref[level].astype(jnp.float32).astype(jnp.bfloat16), split, preferred_element_type=jnp.float32
            ).astype(jnp.int32)
            for y in range(QUAD):
                numbers[y] = spread[:, y * LANES : (y + 1) * LANES]
            for x in range(SUB):
                for y in range(QUAD):
                    index_ref[target + level, x, y] = numbers[y, pl.ds(x, SUB, stride=SUB)] + table_base

    def first_terms(k, carry):
        for g in range(groups):
            for c in range(2):
                basis[g, k, c] = first_ref[g, k, c]
        return carry

    lax.fori_loop(0, terms, first_terms, 0)

    def depth_step(z, carry):
        for x in range(SUB):
            for y in range(QUAD):
                index = index_ref[z, x, y]
                layer = None
                for g in range(groups):
                    real = imag = None
                    for k in range(terms):
                        coef_r = lane_take(table_ref[g, 0, k], index)
                        coef_i = lane_take(table_ref[g, 1, k], index)
                        field_r, field_i = basis[g, k, 0, x, y], basis[g, k, 1, x, y]
                        if k == 0:
                            real = coef_r * field_r - coef_i * field_i
                            imag = coef_r * field_i + coef_i * field_r
                        else:
                            real = real + coef_r * field_r - coef_i * field_i
                            imag = imag + coef_r * field_i + coef_i * field_r
                    basis[g, 0, 0, x, y] = real
                    basis[g, 0, 1, x, y] = imag
                    layer = real if layer is None else layer + real
                layers[z, y, pl.ds(x, SUB, stride=SUB)] = layer * scale

        @pl.when(z < depths - 1)
        def _():
            for g in range(groups):
                for c in range(2):
                    start = [[basis[g, 0, c, x, y] for y in range(QUAD)] for x in range(SUB)]

                    def put(k, x, y, value):
                        basis[g, k, c, x, y] = value

                    chebyshev(start, terms, masks, put)

        return carry

    lax.fori_loop(0, depths, depth_step, 0)

    turned = lax.broadcasted_iota(jnp.int32, (LANES, columns), 0) % ENTRY_SPAN * QUAD
    wanted = lax.broadcasted_iota(jnp.int32, (LANES, columns), 1)
    joins = jnp.concatenate([(wanted == turned + y).astype(jnp.float32).astype(jnp.bfloat16) for y in range(QUAD)], axis=0)
    rows = layers.shape[2]
    chunk = math.gcd(depths, 4)

    def join(step, carry):
        rest = jnp.concatenate(
            [jnp.concatenate([layers[step * chunk + i, y] for y in range(QUAD)], axis=1) for i in range(chunk)], axis=0
        )
        whole = None
        for part in range(2):
            piece = rest.astype(jnp.bfloat16)
            rest = rest - piece.astype(jnp.float32)
            product = jnp.dot(piece, joins, preferred_element_type=jnp.float32)
            whole = product if whole is None else whole + product
        for i in range(chunk):
            z = step * chunk + i
            place = jnp.bitwise_xor(z // levels, depth_pos)
            level = z % levels

            def emit(ref):
                ref[(place // 2) * levels + level] = whole[i * rows : (i + 1) * rows]

            pl.when(place % 2 == 0)(functools.partial(emit, keep_ref))
            pl.when(place % 2 == 1)(functools.partial(emit, send_ref))
        return carry

    lax.fori_loop(0, depths // chunk, join, 0)


def per_device(surface, freq_slot, tap_table, vel_index):
    local_count, _, rows, columns = surface.shape
    depth_count = lax.axis_size("depth")
    freq_count = lax.axis_size("freq")
    levels = vel_index.shape[0]
    _, terms, entries, table_freqs = tap_table.shape
    count = -(-local_count // depth_count)
    groups = -(-count // PAIR)
    depths = depth_count * levels
    vmem = pl.BlockSpec(memory_space=pltpu.VMEM)
    params = pltpu.CompilerParams(vmem_limit_bytes=40 * 1024 * 1024)

    vels = [exchange(vel_index, "depth", flip) for flip in range(1, depth_count)]

    basis_shape = (groups, terms, 2, SUB, QUAD, SUB, LANES)
    hbm = pl.BlockSpec(memory_space=pltpu.HBM)
    table, basis, own_vel = pl.pallas_call(
        functools.partial(first_kernel, (groups, count, local_count, terms, entries)),
        out_shape=(
            jax.ShapeDtypeStruct((groups, 2, terms, SUB, LANES), jnp.float32),
            jax.ShapeDtypeStruct(basis_shape, jnp.float32),
            jax.ShapeDtypeStruct(vel_index.shape, jnp.int32),
        ),
        in_specs=[hbm] * 4,
        out_specs=(vmem, vmem, vmem),
        scratch_shapes=[
            pltpu.VMEM((count, 2, rows, columns), jnp.float32),
            pltpu.SemaphoreType.DMA((count,)),
            pltpu.VMEM((groups, 2, PAIR, 2, rows, LANES), jnp.float32),
            pltpu.SMEM((local_count,), jnp.int32),
            pltpu.VMEM((2 * terms * entries, table_freqs), jnp.float32),
            pltpu.SemaphoreType.DMA((3,)),
        ],
        compiler_params=params,
        cost_estimate=pl.CostEstimate(flops=200_000_000, bytes_accessed=16_000_000, transcendentals=0),
    )(
        *[
            pltpu.with_memory_space_constraint(array, pltpu.HBM)
            for array in (freq_slot, surface, tap_table.reshape(2 * terms * entries, table_freqs), vel_index)
        ]
    )

    scale = 1.0 / math.sqrt(local_count * freq_count)
    half = jax.ShapeDtypeStruct((depths // 2, rows, columns), jnp.float32)
    keep, send = pl.pallas_call(
        functools.partial(image_kernel, (groups, depth_count, levels, terms), scale),
        out_shape=(half, half),
        in_specs=[vmem] * (2 + depth_count),
        out_specs=(vmem, vmem),
        scratch_shapes=[
            pltpu.VMEM((QUAD, rows, LANES), jnp.int32),
            pltpu.VMEM((depths, SUB, QUAD, SUB, LANES), jnp.int32),
            pltpu.VMEM((depths, QUAD, rows, LANES), jnp.float32),
            pltpu.VMEM(basis_shape, jnp.float32),
        ],
        compiler_params=params,
    )(table, basis, own_vel, *vels)

    image = keep + exchange(send, "depth", 1)
    distance = 2
    while distance < depth_count:
        image = image.reshape((-1, 2, levels, rows, columns))
        image = (image[:, 0] + exchange(image[:, 1], "depth", distance)).reshape((-1, rows, columns))
        distance *= 2
    distance = 1
    while distance < freq_count:
        if distance == 1 and freq_count >= 4:
            image = image + exchange(image, "freq", 1) + (exchange(image, "freq", 2) + exchange(image, "freq", 3))
            distance = 4
        else:
            image = image + exchange(image, "freq", distance)
            distance *= 2
    return image


def solution(mesh):
    in_specs = (P("freq", None, None, None), P("freq"), P(), P("depth", None, None))
    out_specs = P("depth", None, None)
    return jax.shard_map(
        per_device, mesh=mesh, in_specs=in_specs, out_specs=out_specs, check_vma=False
    )
```

```python
import functools
import math

import jax
import jax.numpy as jnp
from jax import lax
from jax.experimental import pallas as pl
from jax.experimental.pallas import tpu as pltpu
from jax.sharding import PartitionSpec as P

SUB = 8
LANES = 128
PAIR = 2
QUAD = 4
ENTRY_SPAN = LANES // PAIR


def exchange(value, axis, flip):
    count = lax.axis_size(axis)
    return lax.ppermute(value, axis, [(i, i ^ flip) for i in range(count)])


def lane_take(vector, index):
    return jnp.take_along_axis(vector, index, axis=1, mode="promise_in_bounds")


def lane_number():
    return lax.broadcasted_iota(jnp.int32, (SUB, LANES), 1)


def edge_masks():
    lane = lane_number() % ENTRY_SPAN
    row = lax.broadcasted_iota(jnp.int32, (SUB, LANES), 0)
    return (
        (lane > 0).astype(jnp.float32),
        (lane < ENTRY_SPAN - 1).astype(jnp.float32),
        (row > 0).astype(jnp.float32),
        (row < SUB - 1).astype(jnp.float32),
    )


def chebyshev(start, terms, masks, put):
    left_mask, right_mask, top_mask, bottom_mask = masks
    current, sums = start, None
    for k in range(1, terms):
        lines = []
        for y in range(QUAD):
            column = [current[x][y] for x in range(SUB)]
            above = pltpu.roll(column[SUB - 1], 1, 0) * top_mask
            below = pltpu.roll(column[0], SUB - 1, 0) * bottom_mask
            lines.append([above] + column + [below])
        pairs = [lines[y][0] + lines[y][1] for y in range(QUAD)]
        following, following_sums = [], []
        for x in range(SUB):
            later = [lines[y][x + 1] + lines[y][x + 2] for y in range(QUAD)]
            line = [pairs[y] + later[y] for y in range(QUAD)]
            pairs = later
            left = pltpu.roll(line[QUAD - 1], 1, 1) * left_mask
            right = pltpu.roll(line[0], LANES - 1, 1) * right_mask
            line = [left] + line + [right]
            sides = [line[i] + line[i + 1] for i in range(QUAD + 1)]
            new, new_sums = [], []
            for y in range(QUAD):
                wide = sides[y] + sides[y + 1]
                total = 0.125 * wide if k == 1 else 0.25 * wide - sums[x][y]
                value = total - current[x][y]
                put(k, x, y, value)
                new.append(value)
                new_sums.append(total)
            following.append(new)
            following_sums.append(new_sums)
        current, sums = following, following_sums


def split_index(y):
    return (lane_number() % (LANES // QUAD)) * QUAD + y


def first_kernel(
    sizes, slot_hbm, surface_ref, tap_hbm, vel_hbm, table_ref, basis_ref, vel_ref, raw, raw_sem, halves, slot_ref, tap_ref, sems
):
    groups, count, local_count, terms, entries = sizes
    first = lax.axis_index("depth") * count
    members = [jnp.minimum(first + j, local_count - 1) for j in range(count)]
    slot_copy = pltpu.make_async_copy(slot_hbm, slot_ref, sems.at[0])
    tap_copy = pltpu.make_async_copy(tap_hbm, tap_ref, sems.at[1])
    vel_copy = pltpu.make_async_copy(vel_hbm, vel_ref, sems.at[2])
    copies = [pltpu.make_async_copy(surface_ref.at[members[j]], raw.at[j], raw_sem.at[j]) for j in range(count)]
    slot_copy.start()
    tap_copy.start()
    for copy in copies:
        copy.start()
    vel_copy.start()
    slot_copy.wait()
    tap_copy.wait()

    table_freqs = tap_ref.shape[1]
    rows = -(-count // SUB) * SUB
    freq_lane = lax.broadcasted_iota(jnp.int32, (rows, table_freqs), 1)
    freq_row = lax.broadcasted_iota(jnp.int32, (rows, table_freqs), 0)
    wanted = jnp.zeros((rows, table_freqs), jnp.int32)
    for j in range(count):
        wanted = jnp.where(freq_row == j, slot_ref[members[j]], wanted)
    picked = lax.dot_general(
        (freq_lane == wanted).astype(jnp.float32),
        tap_ref[...],
        (((1,), (1,)), ((), ())),
        precision=lax.Precision.HIGHEST,
        preferred_element_type=jnp.float32,
    )
    lane = lane_number()
    per_vector = LANES // entries
    for g in range(groups):
        for c in range(2):
            for k in range(terms):
                place = c * terms + k
                vector = place // per_vector
                whole = picked[:, vector * LANES : (vector + 1) * LANES]
                if whole.shape[1] < LANES:
                    whole = jnp.concatenate([whole, jnp.zeros((rows, LANES - whole.shape[1]), jnp.float32)], axis=1)
                sides = []
                for i in range(PAIR):
                    turn = ((place % per_vector) * entries - i * ENTRY_SPAN) % LANES
                    turned = pltpu.roll(whole, LANES - turn, 1) if turn else whole
                    j = min(g * PAIR + i, count - 1)
                    sides.append(jnp.broadcast_to(turned[j : j + 1], (SUB, LANES)))
                table_ref[g, c, k] = jnp.where(lane < ENTRY_SPAN, sides[0], sides[1])

    for copy in copies:
        copy.wait()
    masks = edge_masks()
    in_low = lane % ENTRY_SPAN < ENTRY_SPAN // 2
    for g in range(groups):
        for c in range(2):
            for i in range(PAIR):
                j = min(g * PAIR + i, count - 1)
                for h in range(2):
                    halves[g, c, i, h] = raw[j, c, :, h * LANES : (h + 1) * LANES]
    for y in range(QUAD):
        index = split_index(y)
        for g in range(groups):
            for c in range(2):
                for x in range(SUB):
                    sides = []
                    for i in range(PAIR):
                        low, high = [lane_take(halves[g, c, i, h, pl.ds(x, SUB, stride=SUB)], index) for h in range(2)]
                        side = jnp.where(in_low, low, high)
                        j = g * PAIR + i
                        if j >= count:
                            side = jnp.zeros_like(side)
                        elif count * lax.axis_size("depth") > local_count:
                            side = jnp.where(first + j < local_count, side, 0.0)
                        sides.append(side)
                    basis_ref[g, 0, c, x, y] = jnp.where(lane < ENTRY_SPAN, sides[0], sides[1])
    for g in range(groups):
        for c in range(2):
            start = [[basis_ref[g, 0, c, x, y] for y in range(QUAD)] for x in range(SUB)]

            def put(k, x, y, value):
                basis_ref[g, k, c, x, y] = value

            chebyshev(start, terms, masks, put)
    vel_copy.wait()


def image_kernel(sizes, scale, table_ref, first_ref, *refs):
    groups, depth_count, levels, terms = sizes
    vel_refs = refs[:depth_count]
    keep_ref, send_ref, numbers, index_ref, layers, basis = refs[depth_count:]
    depth_pos = lax.axis_index("depth")
    depths = depth_count * levels
    columns = QUAD * ENTRY_SPAN
    masks = edge_masks()

    source = lax.broadcasted_iota(jnp.int32, (columns, QUAD * LANES), 0)
    place = lax.broadcasted_iota(jnp.int32, (columns, QUAD * LANES), 1)
    split = (source == (place % ENTRY_SPAN) * QUAD + place // LANES).astype(jnp.float32).astype(jnp.bfloat16)

    table_base = jnp.where(lane_number() < ENTRY_SPAN, 0, ENTRY_SPAN)
    for slot, vel_ref in enumerate(vel_refs):
        target = jnp.bitwise_xor(depth_pos, slot) * levels
        for level in range(levels):
            spread = jnp.dot(
                vel_ref[level].astype(jnp.float32).astype(jnp.bfloat16), split, preferred_element_type=jnp.float32
            ).astype(jnp.int32)
            for y in range(QUAD):
                numbers[y] = spread[:, y * LANES : (y + 1) * LANES]
            for x in range(SUB):
                for y in range(QUAD):
                    index_ref[target + level, x, y] = numbers[y, pl.ds(x, SUB, stride=SUB)] + table_base

    def first_terms(k, carry):
        for g in range(groups):
            for c in range(2):
                basis[g, k, c] = first_ref[g, k, c]
        return carry

    lax.fori_loop(0, terms, first_terms, 0)

    def depth_step(z, carry):
        for x in range(SUB):
            for y in range(QUAD):
                index = index_ref[z, x, y]
                layer = None
                for g in range(groups):
                    real = imag = None
                    for k in range(terms):
                        coef_r = lane_take(table_ref[g, 0, k], index)
                        coef_i = lane_take(table_ref[g, 1, k], index)
                        field_r, field_i = basis[g, k, 0, x, y], basis[g, k, 1, x, y]
                        if k == 0:
                            real = coef_r * field_r - coef_i * field_i
                            imag = coef_r * field_i + coef_i * field_r
                        else:
                            real = real + coef_r * field_r - coef_i * field_i
                            imag = imag + coef_r * field_i + coef_i * field_r
                    basis[g, 0, 0, x, y] = real
                    basis[g, 0, 1, x, y] = imag
                    layer = real if layer is None else layer + real
                layers[z, y, pl.ds(x, SUB, stride=SUB)] = layer * scale

        @pl.when(z < depths - 1)
        def _():
            for g in range(groups):
                for c in range(2):
                    start = [[basis[g, 0, c, x, y] for y in range(QUAD)] for x in range(SUB)]

                    def put(k, x, y, value):
                        basis[g, k, c, x, y] = value

                    chebyshev(start, terms, masks, put)

        return carry

    lax.fori_loop(0, depths, depth_step, 0)

    turned = lax.broadcasted_iota(jnp.int32, (LANES, columns), 0) % ENTRY_SPAN * QUAD
    wanted = lax.broadcasted_iota(jnp.int32, (LANES, columns), 1)
    joins = jnp.concatenate([(wanted == turned + y).astype(jnp.float32).astype(jnp.bfloat16) for y in range(QUAD)], axis=0)
    rows = layers.shape[2]
    chunk = math.gcd(depths, 4)

    def join(step, carry):
        rest = jnp.concatenate(
            [jnp.concatenate([layers[step * chunk + i, y] for y in range(QUAD)], axis=1) for i in range(chunk)], axis=0
        )
        whole = None
        for part in range(2):
            piece = rest.astype(jnp.bfloat16)
            rest = rest - piece.astype(jnp.float32)
            product = jnp.dot(piece, joins, preferred_element_type=jnp.float32)
            whole = product if whole is None else whole + product
        for i in range(chunk):
            z = step * chunk + i
            place = jnp.bitwise_xor(z // levels, depth_pos)
            level = z % levels

            def emit(ref):
                ref[(place // 2) * levels + level] = whole[i * rows : (i + 1) * rows]

            side = jnp.bitwise_xor(place, place // 2) % 2
            pl.when(side == 0)(functools.partial(emit, keep_ref))
            pl.when(side == 1)(functools.partial(emit, send_ref))
        return carry

    lax.fori_loop(0, depths // chunk, join, 0)


def per_device(surface, freq_slot, tap_table, vel_index):
    local_count, _, rows, columns = surface.shape
    depth_count = lax.axis_size("depth")
    freq_count = lax.axis_size("freq")
    levels = vel_index.shape[0]
    _, terms, entries, table_freqs = tap_table.shape
    count = -(-local_count // depth_count)
    groups = -(-count // PAIR)
    depths = depth_count * levels
    vmem = pl.BlockSpec(memory_space=pltpu.VMEM)
    params = pltpu.CompilerParams(vmem_limit_bytes=40 * 1024 * 1024)

    near = exchange(vel_index, "depth", 1)
    far = [exchange(vel_index, "depth", flip) for flip in range(2, depth_count, 2)]

    basis_shape = (groups, terms, 2, SUB, QUAD, SUB, LANES)
    hbm = pl.BlockSpec(memory_space=pltpu.HBM)
    table, basis, own_vel = pl.pallas_call(
        functools.partial(first_kernel, (groups, count, local_count, terms, entries)),
        out_shape=(
            jax.ShapeDtypeStruct((groups, 2, terms, SUB, LANES), jnp.float32),
            jax.ShapeDtypeStruct(basis_shape, jnp.float32),
            jax.ShapeDtypeStruct(vel_index.shape, jnp.int32),
        ),
        in_specs=[hbm] * 4,
        out_specs=(vmem, vmem, vmem),
        scratch_shapes=[
            pltpu.VMEM((count, 2, rows, columns), jnp.float32),
            pltpu.SemaphoreType.DMA((count,)),
            pltpu.VMEM((groups, 2, PAIR, 2, rows, LANES), jnp.float32),
            pltpu.SMEM((local_count,), jnp.int32),
            pltpu.VMEM((2 * terms * entries, table_freqs), jnp.float32),
            pltpu.SemaphoreType.DMA((3,)),
        ],
        compiler_params=params,
        cost_estimate=pl.CostEstimate(flops=200_000_000, bytes_accessed=16_000_000, transcendentals=0),
    )(
        *[
            pltpu.with_memory_space_constraint(array, pltpu.HBM)
            for array in (freq_slot, surface, tap_table.reshape(2 * terms * entries, table_freqs), vel_index)
        ]
    )

    vels = [near]
    for value in far:
        value, table = lax.optimization_barrier((value, table))
        vels += [value, exchange(value, "depth", 1)]

    scale = 1.0 / math.sqrt(local_count * freq_count)
    half = jax.ShapeDtypeStruct((depths // 2, rows, columns), jnp.float32)
    keep, send = pl.pallas_call(
        functools.partial(image_kernel, (groups, depth_count, levels, terms), scale),
        out_shape=(half, half),
        in_specs=[vmem] * (2 + depth_count),
        out_specs=(vmem, vmem),
        scratch_shapes=[
            pltpu.VMEM((QUAD, rows, LANES), jnp.int32),
            pltpu.VMEM((depths, SUB, QUAD, SUB, LANES), jnp.int32),
            pltpu.VMEM((depths, QUAD, rows, LANES), jnp.float32),
            pltpu.VMEM(basis_shape, jnp.float32),
        ],
        compiler_params=params,
    )(table, basis, own_vel, *vels)

    image = keep + exchange(send, "depth", 1)
    distance = 2
    while distance < depth_count:
        image = image.reshape((-1, 2, levels, rows, columns))
        flip = 3 if distance == 2 else distance
        image = (image[:, 0] + exchange(image[:, 1], "depth", flip)).reshape((-1, rows, columns))
        distance *= 2
    distance = 1
    while distance < freq_count:
        if distance == 1 and freq_count >= 4:
            image = image + exchange(image, "freq", 1) + (exchange(image, "freq", 2) + exchange(image, "freq", 3))
            distance = 4
        else:
            image = image + exchange(image, "freq", distance)
            distance *= 2
    return image


def solution(mesh):
    in_specs = (P("freq", None, None, None), P("freq"), P(), P("depth", None, None))
    out_specs = P("depth", None, None)
    return jax.shard_map(
        per_device, mesh=mesh, in_specs=in_specs, out_specs=out_specs, check_vma=False
    )
```

```python
import functools
import math

import jax
import jax.numpy as jnp
from jax import lax
from jax.experimental import pallas as pl
from jax.experimental.pallas import tpu as pltpu
from jax.sharding import PartitionSpec as P

SUB = 8
LANES = 128
PAIR = 2
QUAD = 4
ENTRY_SPAN = LANES // PAIR
EARLY = 2


def exchange(value, axis, flip):
    count = lax.axis_size(axis)
    return lax.ppermute(value, axis, [(i, i ^ flip) for i in range(count)])


def lane_take(vector, index):
    return jnp.take_along_axis(vector, index, axis=1, mode="promise_in_bounds")


def lane_number():
    return lax.broadcasted_iota(jnp.int32, (SUB, LANES), 1)


def edge_masks():
    lane = lane_number() % ENTRY_SPAN
    row = lax.broadcasted_iota(jnp.int32, (SUB, LANES), 0)
    return (
        (lane > 0).astype(jnp.float32),
        (lane < ENTRY_SPAN - 1).astype(jnp.float32),
        (row > 0).astype(jnp.float32),
        (row < SUB - 1).astype(jnp.float32),
    )


def chebyshev(start, terms, masks, put):
    left_mask, right_mask, top_mask, bottom_mask = masks
    current, sums = start, None
    for k in range(1, terms):
        lines = []
        for y in range(QUAD):
            column = [current[x][y] for x in range(SUB)]
            above = pltpu.roll(column[SUB - 1], 1, 0) * top_mask
            below = pltpu.roll(column[0], SUB - 1, 0) * bottom_mask
            lines.append([above] + column + [below])
        pairs = [lines[y][0] + lines[y][1] for y in range(QUAD)]
        following, following_sums = [], []
        for x in range(SUB):
            later = [lines[y][x + 1] + lines[y][x + 2] for y in range(QUAD)]
            line = [pairs[y] + later[y] for y in range(QUAD)]
            pairs = later
            left = pltpu.roll(line[QUAD - 1], 1, 1) * left_mask
            right = pltpu.roll(line[0], LANES - 1, 1) * right_mask
            line = [left] + line + [right]
            sides = [line[i] + line[i + 1] for i in range(QUAD + 1)]
            new, new_sums = [], []
            for y in range(QUAD):
                wide = sides[y] + sides[y + 1]
                total = 0.125 * wide if k == 1 else 0.25 * wide - sums[x][y]
                value = total - current[x][y]
                put(k, x, y, value)
                new.append(value)
                new_sums.append(total)
            following.append(new)
            following_sums.append(new_sums)
        current, sums = following, following_sums


def split_index(y):
    return (lane_number() % (LANES // QUAD)) * QUAD + y


def first_kernel(
    sizes, slot_hbm, surface_ref, tap_hbm, vel_hbm, table_ref, basis_ref, vel_ref, raw, raw_sem, halves, slot_ref, tap_ref, sems
):
    groups, count, local_count, terms, entries = sizes
    first = lax.axis_index("depth") * count
    members = [jnp.minimum(first + j, local_count - 1) for j in range(count)]
    slot_copy = pltpu.make_async_copy(slot_hbm, slot_ref, sems.at[0])
    tap_copy = pltpu.make_async_copy(tap_hbm, tap_ref, sems.at[1])
    vel_copy = pltpu.make_async_copy(vel_hbm, vel_ref, sems.at[2])
    copies = [pltpu.make_async_copy(surface_ref.at[members[j]], raw.at[j], raw_sem.at[j]) for j in range(count)]
    slot_copy.start()
    tap_copy.start()
    for copy in copies:
        copy.start()
    vel_copy.start()
    slot_copy.wait()
    tap_copy.wait()

    table_freqs = tap_ref.shape[1]
    rows = -(-count // SUB) * SUB
    freq_lane = lax.broadcasted_iota(jnp.int32, (rows, table_freqs), 1)
    freq_row = lax.broadcasted_iota(jnp.int32, (rows, table_freqs), 0)
    wanted = jnp.zeros((rows, table_freqs), jnp.int32)
    for j in range(count):
        wanted = jnp.where(freq_row == j, slot_ref[members[j]], wanted)
    picked = lax.dot_general(
        (freq_lane == wanted).astype(jnp.float32),
        tap_ref[...],
        (((1,), (1,)), ((), ())),
        precision=lax.Precision.HIGHEST,
        preferred_element_type=jnp.float32,
    )
    lane = lane_number()
    per_vector = LANES // entries
    for g in range(groups):
        for c in range(2):
            for k in range(terms):
                place = c * terms + k
                vector = place // per_vector
                whole = picked[:, vector * LANES : (vector + 1) * LANES]
                if whole.shape[1] < LANES:
                    whole = jnp.concatenate([whole, jnp.zeros((rows, LANES - whole.shape[1]), jnp.float32)], axis=1)
                sides = []
                for i in range(PAIR):
                    turn = ((place % per_vector) * entries - i * ENTRY_SPAN) % LANES
                    turned = pltpu.roll(whole, LANES - turn, 1) if turn else whole
                    j = min(g * PAIR + i, count - 1)
                    sides.append(jnp.broadcast_to(turned[j : j + 1], (SUB, LANES)))
                table_ref[g, c, k] = jnp.where(lane < ENTRY_SPAN, sides[0], sides[1])

    for copy in copies:
        copy.wait()
    masks = edge_masks()
    in_low = lane % ENTRY_SPAN < ENTRY_SPAN // 2
    for g in range(groups):
        for c in range(2):
            for i in range(PAIR):
                j = min(g * PAIR + i, count - 1)
                for h in range(2):
                    halves[g, c, i, h] = raw[j, c, :, h * LANES : (h + 1) * LANES]
    for y in range(QUAD):
        index = split_index(y)
        for g in range(groups):
            for c in range(2):
                for x in range(SUB):
                    sides = []
                    for i in range(PAIR):
                        low, high = [lane_take(halves[g, c, i, h, pl.ds(x, SUB, stride=SUB)], index) for h in range(2)]
                        side = jnp.where(in_low, low, high)
                        j = g * PAIR + i
                        if j >= count:
                            side = jnp.zeros_like(side)
                        elif count * lax.axis_size("depth") > local_count:
                            side = jnp.where(first + j < local_count, side, 0.0)
                        sides.append(side)
                    basis_ref[g, 0, c, x, y] = jnp.where(lane < ENTRY_SPAN, sides[0], sides[1])
    for g in range(groups):
        for c in range(2):
            start = [[basis_ref[g, 0, c, x, y] for y in range(QUAD)] for x in range(SUB)]

            def put(k, x, y, value):
                basis_ref[g, k, c, x, y] = value

            chebyshev(start, terms, masks, put)
    vel_copy.wait()


def place_velocities(vel_refs, targets, numbers, index_ref):
    columns = QUAD * ENTRY_SPAN
    source = lax.broadcasted_iota(jnp.int32, (columns, QUAD * LANES), 0)
    place = lax.broadcasted_iota(jnp.int32, (columns, QUAD * LANES), 1)
    split = (source == (place % ENTRY_SPAN) * QUAD + place // LANES).astype(jnp.float32).astype(jnp.bfloat16)
    table_base = jnp.where(lane_number() < ENTRY_SPAN, 0, ENTRY_SPAN)
    for vel_ref, target in zip(vel_refs, targets):
        for level in range(vel_ref.shape[0]):
            spread = jnp.dot(
                vel_ref[level].astype(jnp.float32).astype(jnp.bfloat16), split, preferred_element_type=jnp.float32
            ).astype(jnp.int32)
            for y in range(QUAD):
                numbers[y] = spread[:, y * LANES : (y + 1) * LANES]
            for x in range(SUB):
                for y in range(QUAD):
                    index_ref[target + level, x, y] = numbers[y, pl.ds(x, SUB, stride=SUB)] + table_base


def early_kernel(sizes, table_ref, *refs):
    groups, levels, terms = sizes
    vel_refs = refs[:-3]
    coef_ref, numbers, index_ref = refs[-3:]
    place_velocities(vel_refs, [slot * levels for slot in range(len(vel_refs))], numbers, index_ref)
    for z in range(len(vel_refs) * levels):
        for x in range(SUB):
            for y in range(QUAD):
                index = index_ref[z, x, y]
                for g in range(groups):
                    for c in range(2):
                        for k in range(terms):
                            coef_ref[z, g, c, k, x, y] = lane_take(table_ref[g, c, k], index)


def image_kernel(sizes, scale, table_ref, first_ref, coef_ref, *refs):
    groups, depth_count, levels, terms = sizes
    early = coef_ref.shape[0] // levels
    vel_refs = refs[: depth_count - early]
    keep_ref, send_ref, numbers, index_ref, layers, basis = refs[depth_count - early :]
    depth_pos = lax.axis_index("depth")
    depths = depth_count * levels
    columns = QUAD * ENTRY_SPAN
    masks = edge_masks()

    targets = [jnp.bitwise_xor(depth_pos, slot) * levels for slot in range(early, depth_count)]
    place_velocities(vel_refs, targets, numbers, index_ref)

    def first_terms(k, carry):
        for g in range(groups):
            for c in range(2):
                basis[g, k, c] = first_ref[g, k, c]
        return carry

    lax.fori_loop(0, terms, first_terms, 0)

    def accumulate(z, coefficients):
        for x in range(SUB):
            for y in range(QUAD):
                coefficient = coefficients(x, y)
                layer = None
                for g in range(groups):
                    real = imag = None
                    for k in range(terms):
                        coef_r, coef_i = coefficient(g, 0, k), coefficient(g, 1, k)
                        field_r, field_i = basis[g, k, 0, x, y], basis[g, k, 1, x, y]
                        if k == 0:
                            real = coef_r * field_r - coef_i * field_i
                            imag = coef_r * field_i + coef_i * field_r
                        else:
                            real = real + coef_r * field_r - coef_i * field_i
                            imag = imag + coef_r * field_i + coef_i * field_r
                    basis[g, 0, 0, x, y] = real
                    basis[g, 0, 1, x, y] = imag
                    layer = real if layer is None else layer + real
                layers[z, y, pl.ds(x, SUB, stride=SUB)] = layer * scale

    def depth_step(z, carry):
        slot = jnp.bitwise_xor(z // levels, depth_pos)

        @pl.when(slot < early)
        def _():
            at = slot * levels + z % levels
            accumulate(z, lambda x, y: lambda g, c, k: coef_ref[at, g, c, k, x, y])

        @pl.when(slot >= early)
        def _():
            def look_up(x, y):
                index = index_ref[z, x, y]
                return lambda g, c, k: lane_take(table_ref[g, c, k], index)

            accumulate(z, look_up)

        @pl.when(z < depths - 1)
        def _():
            for g in range(groups):
                for c in range(2):
                    start = [[basis[g, 0, c, x, y] for y in range(QUAD)] for x in range(SUB)]

                    def put(k, x, y, value):
                        basis[g, k, c, x, y] = value

                    chebyshev(start, terms, masks, put)

        return carry

    lax.fori_loop(0, depths, depth_step, 0)

    turned = lax.broadcasted_iota(jnp.int32, (LANES, columns), 0) % ENTRY_SPAN * QUAD
    wanted = lax.broadcasted_iota(jnp.int32, (LANES, columns), 1)
    joins = jnp.concatenate([(wanted == turned + y).astype(jnp.float32).astype(jnp.bfloat16) for y in range(QUAD)], axis=0)
    rows = layers.shape[2]
    chunk = math.gcd(depths, 4)

    def join(step, carry):
        rest = jnp.concatenate(
            [jnp.concatenate([layers[step * chunk + i, y] for y in range(QUAD)], axis=1) for i in range(chunk)], axis=0
        )
        whole = None
        for part in range(2):
            piece = rest.astype(jnp.bfloat16)
            rest = rest - piece.astype(jnp.float32)
            product = jnp.dot(piece, joins, preferred_element_type=jnp.float32)
            whole = product if whole is None else whole + product
        for i in range(chunk):
            z = step * chunk + i
            place = jnp.bitwise_xor(z // levels, depth_pos)
            level = z % levels

            def emit(ref):
                ref[(place // 2) * levels + level] = whole[i * rows : (i + 1) * rows]

            side = jnp.bitwise_xor(place, place // 2) % 2
            pl.when(side == 0)(functools.partial(emit, keep_ref))
            pl.when(side == 1)(functools.partial(emit, send_ref))
        return carry

    lax.fori_loop(0, depths // chunk, join, 0)


def per_device(surface, freq_slot, tap_table, vel_index):
    local_count, _, rows, columns = surface.shape
    depth_count = lax.axis_size("depth")
    freq_count = lax.axis_size("freq")
    levels = vel_index.shape[0]
    _, terms, entries, table_freqs = tap_table.shape
    count = -(-local_count // depth_count)
    groups = -(-count // PAIR)
    depths = depth_count * levels
    vmem = pl.BlockSpec(memory_space=pltpu.VMEM)
    params = pltpu.CompilerParams(vmem_limit_bytes=40 * 1024 * 1024)

    near = exchange(vel_index, "depth", 1)
    far = [exchange(vel_index, "depth", flip) for flip in range(2, depth_count, 2)]

    basis_shape = (groups, terms, 2, SUB, QUAD, SUB, LANES)
    hbm = pl.BlockSpec(memory_space=pltpu.HBM)
    table, basis, own_vel = pl.pallas_call(
        functools.partial(first_kernel, (groups, count, local_count, terms, entries)),
        out_shape=(
            jax.ShapeDtypeStruct((groups, 2, terms, SUB, LANES), jnp.float32),
            jax.ShapeDtypeStruct(basis_shape, jnp.float32),
            jax.ShapeDtypeStruct(vel_index.shape, jnp.int32),
        ),
        in_specs=[hbm] * 4,
        out_specs=(vmem, vmem, vmem),
        scratch_shapes=[
            pltpu.VMEM((count, 2, rows, columns), jnp.float32),
            pltpu.SemaphoreType.DMA((count,)),
            pltpu.VMEM((groups, 2, PAIR, 2, rows, LANES), jnp.float32),
            pltpu.SMEM((local_count,), jnp.int32),
            pltpu.VMEM((2 * terms * entries, table_freqs), jnp.float32),
            pltpu.SemaphoreType.DMA((3,)),
        ],
        compiler_params=params,
        cost_estimate=pl.CostEstimate(flops=200_000_000, bytes_accessed=16_000_000, transcendentals=0),
    )(
        *[
            pltpu.with_memory_space_constraint(array, pltpu.HBM)
            for array in (freq_slot, surface, tap_table.reshape(2 * terms * entries, table_freqs), vel_index)
        ]
    )

    vels = [own_vel, near]
    for value in far:
        value, table = lax.optimization_barrier((value, table))
        vels += [value, exchange(value, "depth", 1)]

    scale = 1.0 / math.sqrt(local_count * freq_count)
    half = jax.ShapeDtypeStruct((depths // 2, rows, columns), jnp.float32)
    early = vels[:EARLY]
    coefs = pl.pallas_call(
        functools.partial(early_kernel, (groups, levels, terms)),
        out_shape=jax.ShapeDtypeStruct((len(early) * levels, groups, 2, terms, SUB, QUAD, SUB, LANES), jnp.float32),
        in_specs=[vmem] * (1 + len(early)),
        out_specs=vmem,
        scratch_shapes=[
            pltpu.VMEM((QUAD, rows, LANES), jnp.int32),
            pltpu.VMEM((len(early) * levels, SUB, QUAD, SUB, LANES), jnp.int32),
        ],
        compiler_params=params,
        cost_estimate=pl.CostEstimate(flops=200_000_000, bytes_accessed=16_000_000, transcendentals=0),
    )(table, *early)

    keep, send = pl.pallas_call(
        functools.partial(image_kernel, (groups, depth_count, levels, terms), scale),
        out_shape=(half, half),
        in_specs=[vmem] * (3 + depth_count - EARLY),
        out_specs=(vmem, vmem),
        scratch_shapes=[
            pltpu.VMEM((QUAD, rows, LANES), jnp.int32),
            pltpu.VMEM((depths, SUB, QUAD, SUB, LANES), jnp.int32),
            pltpu.VMEM((depths, QUAD, rows, LANES), jnp.float32),
            pltpu.VMEM(basis_shape, jnp.float32),
        ],
        compiler_params=params,
    )(table, basis, coefs, *vels[EARLY:])

    image = keep + exchange(send, "depth", 1)
    distance = 2
    while distance < depth_count:
        image = image.reshape((-1, 2, levels, rows, columns))
        flip = 3 if distance == 2 else distance
        image = (image[:, 0] + exchange(image[:, 1], "depth", flip)).reshape((-1, rows, columns))
        distance *= 2
    distance = 1
    while distance < freq_count:
        if distance == 1 and freq_count >= 4:
            image = image + exchange(image, "freq", 1) + (exchange(image, "freq", 2) + exchange(image, "freq", 3))
            distance = 4
        else:
            image = image + exchange(image, "freq", distance)
            distance *= 2
    return image


def solution(mesh):
    in_specs = (P("freq", None, None, None), P("freq"), P(), P("depth", None, None))
    out_specs = P("depth", None, None)
    return jax.shard_map(
        per_device, mesh=mesh, in_specs=in_specs, out_specs=out_specs, check_vma=False
    )
```

```python
import functools
import math

import jax
import jax.numpy as jnp
from jax import lax
from jax.experimental import pallas as pl
from jax.experimental.pallas import tpu as pltpu
from jax.sharding import PartitionSpec as P

SUB = 8
LANES = 128
PAIR = 2
QUAD = 4
ENTRY_SPAN = LANES // PAIR
EARLY = 2


def exchange(value, axis, flip):
    count = lax.axis_size(axis)
    return lax.ppermute(value, axis, [(i, i ^ flip) for i in range(count)])


def lane_take(vector, index):
    return jnp.take_along_axis(vector, index, axis=1, mode="promise_in_bounds")


def lane_number():
    return lax.broadcasted_iota(jnp.int32, (SUB, LANES), 1)


def edge_masks():
    lane = lane_number() % ENTRY_SPAN
    row = lax.broadcasted_iota(jnp.int32, (SUB, LANES), 0)
    return (
        (lane > 0).astype(jnp.float32),
        (lane < ENTRY_SPAN - 1).astype(jnp.float32),
        (row > 0).astype(jnp.float32),
        (row < SUB - 1).astype(jnp.float32),
    )


def chebyshev(start, terms, masks, put):
    left_mask, right_mask, top_mask, bottom_mask = masks
    current, sums = start, None
    for k in range(1, terms):
        lines = []
        for y in range(QUAD):
            column = [current[x][y] for x in range(SUB)]
            above = pltpu.roll(column[SUB - 1], 1, 0) * top_mask
            below = pltpu.roll(column[0], SUB - 1, 0) * bottom_mask
            lines.append([above] + column + [below])
        pairs = [lines[y][0] + lines[y][1] for y in range(QUAD)]
        following, following_sums = [], []
        for x in range(SUB):
            later = [lines[y][x + 1] + lines[y][x + 2] for y in range(QUAD)]
            line = [pairs[y] + later[y] for y in range(QUAD)]
            pairs = later
            left = pltpu.roll(line[QUAD - 1], 1, 1) * left_mask
            right = pltpu.roll(line[0], LANES - 1, 1) * right_mask
            line = [left] + line + [right]
            sides = [line[i] + line[i + 1] for i in range(QUAD + 1)]
            new, new_sums = [], []
            for y in range(QUAD):
                wide = sides[y] + sides[y + 1]
                total = 0.125 * wide if k == 1 else 0.25 * wide - sums[x][y]
                value = total - current[x][y]
                put(k, x, y, value)
                new.append(value)
                new_sums.append(total)
            following.append(new)
            following_sums.append(new_sums)
        current, sums = following, following_sums


def split_index(y):
    return (lane_number() % (LANES // QUAD)) * QUAD + y


def first_kernel(
    sizes, slot_hbm, surface_ref, tap_hbm, vel_hbm, table_ref, basis_ref, vel_ref, raw, raw_sem, halves, slot_ref, tap_ref, sems
):
    groups, count, local_count, terms, entries = sizes
    first = lax.axis_index("depth") * count
    members = [jnp.minimum(first + j, local_count - 1) for j in range(count)]
    slot_copy = pltpu.make_async_copy(slot_hbm, slot_ref, sems.at[0])
    tap_copy = pltpu.make_async_copy(tap_hbm, tap_ref, sems.at[1])
    vel_copy = pltpu.make_async_copy(vel_hbm, vel_ref, sems.at[2])
    copies = [pltpu.make_async_copy(surface_ref.at[members[j]], raw.at[j], raw_sem.at[j]) for j in range(count)]
    slot_copy.start()
    tap_copy.start()
    for copy in copies:
        copy.start()
    vel_copy.start()
    slot_copy.wait()
    tap_copy.wait()

    table_freqs = tap_ref.shape[1]
    rows = -(-count // SUB) * SUB
    freq_lane = lax.broadcasted_iota(jnp.int32, (rows, table_freqs), 1)
    freq_row = lax.broadcasted_iota(jnp.int32, (rows, table_freqs), 0)
    wanted = jnp.zeros((rows, table_freqs), jnp.int32)
    for j in range(count):
        wanted = jnp.where(freq_row == j, slot_ref[members[j]], wanted)
    picked = lax.dot_general(
        (freq_lane == wanted).astype(jnp.float32),
        tap_ref[...],
        (((1,), (1,)), ((), ())),
        precision=lax.Precision.HIGHEST,
        preferred_element_type=jnp.float32,
    )
    lane = lane_number()
    per_vector = LANES // entries
    for g in range(groups):
        for c in range(2):
            for k in range(terms):
                place = c * terms + k
                vector = place // per_vector
                whole = picked[:, vector * LANES : (vector + 1) * LANES]
                if whole.shape[1] < LANES:
                    whole = jnp.concatenate([whole, jnp.zeros((rows, LANES - whole.shape[1]), jnp.float32)], axis=1)
                sides = []
                for i in range(PAIR):
                    turn = ((place % per_vector) * entries - i * ENTRY_SPAN) % LANES
                    turned = pltpu.roll(whole, LANES - turn, 1) if turn else whole
                    j = min(g * PAIR + i, count - 1)
                    sides.append(jnp.broadcast_to(turned[j : j + 1], (SUB, LANES)))
                table_ref[g, c, k] = jnp.where(lane < ENTRY_SPAN, sides[0], sides[1])

    for copy in copies:
        copy.wait()
    masks = edge_masks()
    in_low = lane % ENTRY_SPAN < ENTRY_SPAN // 2
    for g in range(groups):
        for c in range(2):
            for i in range(PAIR):
                j = min(g * PAIR + i, count - 1)
                for h in range(2):
                    halves[g, c, i, h] = raw[j, c, :, h * LANES : (h + 1) * LANES]
    for y in range(QUAD):
        index = split_index(y)
        for g in range(groups):
            for c in range(2):
                for x in range(SUB):
                    sides = []
                    for i in range(PAIR):
                        low, high = [lane_take(halves[g, c, i, h, pl.ds(x, SUB, stride=SUB)], index) for h in range(2)]
                        side = jnp.where(in_low, low, high)
                        j = g * PAIR + i
                        if j >= count:
                            side = jnp.zeros_like(side)
                        elif count * lax.axis_size("depth") > local_count:
                            side = jnp.where(first + j < local_count, side, 0.0)
                        sides.append(side)
                    basis_ref[g, 0, c, x, y] = jnp.where(lane < ENTRY_SPAN, sides[0], sides[1])
    for g in range(groups):
        for c in range(2):
            start = [[basis_ref[g, 0, c, x, y] for y in range(QUAD)] for x in range(SUB)]

            def put(k, x, y, value):
                basis_ref[g, k, c, x, y] = value

            chebyshev(start, terms, masks, put)
    vel_copy.wait()


def place_velocities(vel_refs, targets, numbers, index_ref):
    columns = QUAD * ENTRY_SPAN
    source = lax.broadcasted_iota(jnp.int32, (columns, QUAD * LANES), 0)
    place = lax.broadcasted_iota(jnp.int32, (columns, QUAD * LANES), 1)
    split = (source == (place % ENTRY_SPAN) * QUAD + place // LANES).astype(jnp.float32).astype(jnp.bfloat16)
    table_base = jnp.where(lane_number() < ENTRY_SPAN, 0, ENTRY_SPAN)
    for vel_ref, target in zip(vel_refs, targets):
        for level in range(vel_ref.shape[0]):
            spread = jnp.dot(
                vel_ref[level].astype(jnp.float32).astype(jnp.bfloat16), split, preferred_element_type=jnp.float32
            ).astype(jnp.int32)
            for y in range(QUAD):
                numbers[y] = spread[:, y * LANES : (y + 1) * LANES]
            for x in range(SUB):
                for y in range(QUAD):
                    index_ref[target + level, x, y] = numbers[y, pl.ds(x, SUB, stride=SUB)] + table_base


def early_kernel(sizes, table_ref, *refs):
    groups, levels, terms = sizes
    vel_refs = refs[:-3]
    coef_ref, numbers, index_ref = refs[-3:]
    place_velocities(vel_refs, [slot * levels for slot in range(len(vel_refs))], numbers, index_ref)
    for z in range(len(vel_refs) * levels):
        for x in range(SUB):
            for y in range(QUAD):
                index = index_ref[z, x, y]
                for g in range(groups):
                    for c in range(2):
                        for k in range(terms):
                            coef_ref[z, g, c, k, x, y] = lane_take(table_ref[g, c, k], index)


def image_kernel(sizes, scale, table_ref, first_ref, coef_ref, *refs):
    groups, depth_count, levels, terms = sizes
    early = coef_ref.shape[0] // levels
    vel_refs = refs[: depth_count - early]
    keep_ref, send_ref, numbers, index_ref, layers, basis = refs[depth_count - early :]
    depth_pos = lax.axis_index("depth")
    depths = depth_count * levels
    columns = QUAD * ENTRY_SPAN
    masks = edge_masks()

    targets = [jnp.bitwise_xor(depth_pos, slot) * levels for slot in range(early, depth_count)]
    place_velocities(vel_refs, targets, numbers, index_ref)

    def accumulate(z, coefficients, source):
        for x in range(SUB):
            for y in range(QUAD):
                coefficient = coefficients(x, y)
                layer = None
                for g in range(groups):
                    real = imag = None
                    for k in range(terms):
                        coef_r, coef_i = coefficient(g, 0, k), coefficient(g, 1, k)
                        field_r, field_i = source[g, k, 0, x, y], source[g, k, 1, x, y]
                        if k == 0:
                            real = coef_r * field_r - coef_i * field_i
                            imag = coef_r * field_i + coef_i * field_r
                        else:
                            real = real + coef_r * field_r - coef_i * field_i
                            imag = imag + coef_r * field_i + coef_i * field_r
                    basis[g, 0, 0, x, y] = real
                    basis[g, 0, 1, x, y] = imag
                    layer = real if layer is None else layer + real
                layers[z, y, pl.ds(x, SUB, stride=SUB)] = layer * scale

    def image_of(z, source):
        slot = jnp.bitwise_xor(z // levels, depth_pos)

        @pl.when(slot < early)
        def _():
            at = slot * levels + z % levels
            accumulate(z, lambda x, y: lambda g, c, k: coef_ref[at, g, c, k, x, y], source)

        @pl.when(slot >= early)
        def _():
            def look_up(x, y):
                index = index_ref[z, x, y]
                return lambda g, c, k: lane_take(table_ref[g, c, k], index)

            accumulate(z, look_up, source)

    def depth_step(z, carry):
        for g in range(groups):
            for c in range(2):
                start = [[basis[g, 0, c, x, y] for y in range(QUAD)] for x in range(SUB)]

                def put(k, x, y, value):
                    basis[g, k, c, x, y] = value

                chebyshev(start, terms, masks, put)
        image_of(z, basis)
        return carry

    image_of(0, first_ref)
    lax.fori_loop(1, depths, depth_step, 0)

    turned = lax.broadcasted_iota(jnp.int32, (LANES, columns), 0) % ENTRY_SPAN * QUAD
    wanted = lax.broadcasted_iota(jnp.int32, (LANES, columns), 1)
    joins = jnp.concatenate([(wanted == turned + y).astype(jnp.float32).astype(jnp.bfloat16) for y in range(QUAD)], axis=0)
    rows = layers.shape[2]
    chunk = math.gcd(depths, 4)

    def join(step, carry):
        rest = jnp.concatenate(
            [jnp.concatenate([layers[step * chunk + i, y] for y in range(QUAD)], axis=1) for i in range(chunk)], axis=0
        )
        whole = None
        for part in range(2):
            piece = rest.astype(jnp.bfloat16)
            rest = rest - piece.astype(jnp.float32)
            product = jnp.dot(piece, joins, preferred_element_type=jnp.float32)
            whole = product if whole is None else whole + product
        for i in range(chunk):
            z = step * chunk + i
            place = jnp.bitwise_xor(z // levels, depth_pos)
            level = z % levels

            def emit(ref):
                ref[(place // 2) * levels + level] = whole[i * rows : (i + 1) * rows]

            side = jnp.bitwise_xor(place, place // 2) % 2
            pl.when(side == 0)(functools.partial(emit, keep_ref))
            pl.when(side == 1)(functools.partial(emit, send_ref))
        return carry

    lax.fori_loop(0, depths // chunk, join, 0)


def per_device(surface, freq_slot, tap_table, vel_index):
    local_count, _, rows, columns = surface.shape
    depth_count = lax.axis_size("depth")
    freq_count = lax.axis_size("freq")
    levels = vel_index.shape[0]
    _, terms, entries, table_freqs = tap_table.shape
    count = -(-local_count // depth_count)
    groups = -(-count // PAIR)
    depths = depth_count * levels
    vmem = pl.BlockSpec(memory_space=pltpu.VMEM)
    params = pltpu.CompilerParams(vmem_limit_bytes=40 * 1024 * 1024)

    near = exchange(vel_index, "depth", 1)
    far = [exchange(vel_index, "depth", flip) for flip in range(2, depth_count, 2)]

    basis_shape = (groups, terms, 2, SUB, QUAD, SUB, LANES)
    hbm = pl.BlockSpec(memory_space=pltpu.HBM)
    table, basis, own_vel = pl.pallas_call(
        functools.partial(first_kernel, (groups, count, local_count, terms, entries)),
        out_shape=(
            jax.ShapeDtypeStruct((groups, 2, terms, SUB, LANES), jnp.float32),
            jax.ShapeDtypeStruct(basis_shape, jnp.float32),
            jax.ShapeDtypeStruct(vel_index.shape, jnp.int32),
        ),
        in_specs=[hbm] * 4,
        out_specs=(vmem, vmem, vmem),
        scratch_shapes=[
            pltpu.VMEM((count, 2, rows, columns), jnp.float32),
            pltpu.SemaphoreType.DMA((count,)),
            pltpu.VMEM((groups, 2, PAIR, 2, rows, LANES), jnp.float32),
            pltpu.SMEM((local_count,), jnp.int32),
            pltpu.VMEM((2 * terms * entries, table_freqs), jnp.float32),
            pltpu.SemaphoreType.DMA((3,)),
        ],
        compiler_params=params,
        cost_estimate=pl.CostEstimate(flops=200_000_000, bytes_accessed=16_000_000, transcendentals=0),
    )(
        *[
            pltpu.with_memory_space_constraint(array, pltpu.HBM)
            for array in (freq_slot, surface, tap_table.reshape(2 * terms * entries, table_freqs), vel_index)
        ]
    )

    vels = [own_vel, near]
    for value in far:
        value, table = lax.optimization_barrier((value, table))
        vels += [value, exchange(value, "depth", 1)]

    scale = 1.0 / math.sqrt(local_count * freq_count)
    half = jax.ShapeDtypeStruct((depths // 2, rows, columns), jnp.float32)
    early = vels[:EARLY]
    coefs = pl.pallas_call(
        functools.partial(early_kernel, (groups, levels, terms)),
        out_shape=jax.ShapeDtypeStruct((len(early) * levels, groups, 2, terms, SUB, QUAD, SUB, LANES), jnp.float32),
        in_specs=[vmem] * (1 + len(early)),
        out_specs=vmem,
        scratch_shapes=[
            pltpu.VMEM((QUAD, rows, LANES), jnp.int32),
            pltpu.VMEM((len(early) * levels, SUB, QUAD, SUB, LANES), jnp.int32),
        ],
        compiler_params=params,
        cost_estimate=pl.CostEstimate(flops=200_000_000, bytes_accessed=16_000_000, transcendentals=0),
    )(table, *early)

    keep, send = pl.pallas_call(
        functools.partial(image_kernel, (groups, depth_count, levels, terms), scale),
        out_shape=(half, half),
        in_specs=[vmem] * (3 + depth_count - EARLY),
        out_specs=(vmem, vmem),
        scratch_shapes=[
            pltpu.VMEM((QUAD, rows, LANES), jnp.int32),
            pltpu.VMEM((depths, SUB, QUAD, SUB, LANES), jnp.int32),
            pltpu.VMEM((depths, QUAD, rows, LANES), jnp.float32),
            pltpu.VMEM(basis_shape, jnp.float32),
        ],
        compiler_params=params,
    )(table, basis, coefs, *vels[EARLY:])

    image = keep + exchange(send, "depth", 1)
    distance = 2
    while distance < depth_count:
        image = image.reshape((-1, 2, levels, rows, columns))
        flip = 3 if distance == 2 else distance
        image = (image[:, 0] + exchange(image[:, 1], "depth", flip)).reshape((-1, rows, columns))
        distance *= 2
    distance = 1
    while distance < freq_count:
        if distance == 1 and freq_count >= 4:
            image = image + exchange(image, "freq", 1) + (exchange(image, "freq", 2) + exchange(image, "freq", 3))
            distance = 4
        else:
            image = image + exchange(image, "freq", distance)
            distance *= 2
    return image


def solution(mesh):
    in_specs = (P("freq", None, None, None), P("freq"), P(), P("depth", None, None))
    out_specs = P("depth", None, None)
    return jax.shard_map(
        per_device, mesh=mesh, in_specs=in_specs, out_specs=out_specs, check_vma=False
    )
```

```python
import functools
import math

import jax
import jax.numpy as jnp
from jax import lax
from jax.experimental import pallas as pl
from jax.experimental.pallas import tpu as pltpu
from jax.sharding import PartitionSpec as P

SUB = 8
LANES = 128
PAIR = 2
QUAD = 4
ENTRY_SPAN = LANES // PAIR
READY = 6
EARLY = 2


def exchange(value, axis, flip):
    count = lax.axis_size(axis)
    return lax.ppermute(value, axis, [(i, i ^ flip) for i in range(count)])


def lane_take(vector, index):
    return jnp.take_along_axis(vector, index, axis=1, mode="promise_in_bounds")


def lane_number():
    return lax.broadcasted_iota(jnp.int32, (SUB, LANES), 1)


def edge_masks():
    lane = lane_number() % ENTRY_SPAN
    row = lax.broadcasted_iota(jnp.int32, (SUB, LANES), 0)
    return (
        (lane > 0).astype(jnp.float32),
        (lane < ENTRY_SPAN - 1).astype(jnp.float32),
        (row > 0).astype(jnp.float32),
        (row < SUB - 1).astype(jnp.float32),
    )


def chebyshev(start, terms, masks, put):
    left_mask, right_mask, top_mask, bottom_mask = masks
    current, sums = start, None
    for k in range(1, terms):
        lines = []
        for y in range(QUAD):
            column = [current[x][y] for x in range(SUB)]
            above = pltpu.roll(column[SUB - 1], 1, 0) * top_mask
            below = pltpu.roll(column[0], SUB - 1, 0) * bottom_mask
            lines.append([above] + column + [below])
        pairs = [lines[y][0] + lines[y][1] for y in range(QUAD)]
        following, following_sums = [], []
        for x in range(SUB):
            later = [lines[y][x + 1] + lines[y][x + 2] for y in range(QUAD)]
            line = [pairs[y] + later[y] for y in range(QUAD)]
            pairs = later
            left = pltpu.roll(line[QUAD - 1], 1, 1) * left_mask
            right = pltpu.roll(line[0], LANES - 1, 1) * right_mask
            line = [left] + line + [right]
            sides = [line[i] + line[i + 1] for i in range(QUAD + 1)]
            new, new_sums = [], []
            for y in range(QUAD):
                wide = sides[y] + sides[y + 1]
                total = 0.125 * wide if k == 1 else 0.25 * wide - sums[x][y]
                value = total - current[x][y]
                put(k, x, y, value)
                new.append(value)
                new_sums.append(total)
            following.append(new)
            following_sums.append(new_sums)
        current, sums = following, following_sums


def split_index(y):
    return (lane_number() % (LANES // QUAD)) * QUAD + y


def first_kernel(
    sizes, slot_hbm, surface_ref, tap_hbm, vel_hbm, table_ref, basis_ref, vel_ref, raw, raw_sem, halves, slot_ref, tap_ref, sems
):
    groups, count, local_count, terms, entries = sizes
    first = lax.axis_index("depth") * count
    members = [jnp.minimum(first + j, local_count - 1) for j in range(count)]
    slot_copy = pltpu.make_async_copy(slot_hbm, slot_ref, sems.at[0])
    tap_copy = pltpu.make_async_copy(tap_hbm, tap_ref, sems.at[1])
    vel_copy = pltpu.make_async_copy(vel_hbm, vel_ref, sems.at[2])
    copies = [pltpu.make_async_copy(surface_ref.at[members[j]], raw.at[j], raw_sem.at[j]) for j in range(count)]
    slot_copy.start()
    tap_copy.start()
    for copy in copies:
        copy.start()
    vel_copy.start()
    slot_copy.wait()
    tap_copy.wait()

    table_freqs = tap_ref.shape[1]
    rows = -(-count // SUB) * SUB
    freq_lane = lax.broadcasted_iota(jnp.int32, (rows, table_freqs), 1)
    freq_row = lax.broadcasted_iota(jnp.int32, (rows, table_freqs), 0)
    wanted = jnp.zeros((rows, table_freqs), jnp.int32)
    for j in range(count):
        wanted = jnp.where(freq_row == j, slot_ref[members[j]], wanted)
    picked = lax.dot_general(
        (freq_lane == wanted).astype(jnp.float32),
        tap_ref[...],
        (((1,), (1,)), ((), ())),
        precision=lax.Precision.HIGHEST,
        preferred_element_type=jnp.float32,
    )
    lane = lane_number()
    per_vector = LANES // entries
    for g in range(groups):
        for c in range(2):
            for k in range(terms):
                place = c * terms + k
                vector = place // per_vector
                whole = picked[:, vector * LANES : (vector + 1) * LANES]
                if whole.shape[1] < LANES:
                    whole = jnp.concatenate([whole, jnp.zeros((rows, LANES - whole.shape[1]), jnp.float32)], axis=1)
                sides = []
                for i in range(PAIR):
                    turn = ((place % per_vector) * entries - i * ENTRY_SPAN) % LANES
                    turned = pltpu.roll(whole, LANES - turn, 1) if turn else whole
                    j = min(g * PAIR + i, count - 1)
                    sides.append(jnp.broadcast_to(turned[j : j + 1], (SUB, LANES)))
                table_ref[g, c, k] = jnp.where(lane < ENTRY_SPAN, sides[0], sides[1])

    for copy in copies:
        copy.wait()
    masks = edge_masks()
    in_low = lane % ENTRY_SPAN < ENTRY_SPAN // 2
    for g in range(groups):
        for c in range(2):
            for i in range(PAIR):
                j = min(g * PAIR + i, count - 1)
                for h in range(2):
                    halves[g, c, i, h] = raw[j, c, :, h * LANES : (h + 1) * LANES]
    for y in range(QUAD):
        index = split_index(y)
        for g in range(groups):
            for c in range(2):
                for x in range(SUB):
                    sides = []
                    for i in range(PAIR):
                        low, high = [lane_take(halves[g, c, i, h, pl.ds(x, SUB, stride=SUB)], index) for h in range(2)]
                        side = jnp.where(in_low, low, high)
                        j = g * PAIR + i
                        if j >= count:
                            side = jnp.zeros_like(side)
                        elif count * lax.axis_size("depth") > local_count:
                            side = jnp.where(first + j < local_count, side, 0.0)
                        sides.append(side)
                    basis_ref[g, 0, c, x, y] = jnp.where(lane < ENTRY_SPAN, sides[0], sides[1])
    for g in range(groups):
        for c in range(2):
            start = [[basis_ref[g, 0, c, x, y] for y in range(QUAD)] for x in range(SUB)]

            def put(k, x, y, value):
                basis_ref[g, k, c, x, y] = value

            chebyshev(start, terms, masks, put)
    vel_copy.wait()


def place_velocities(vel_refs, targets, numbers, index_ref):
    columns = QUAD * ENTRY_SPAN
    source = lax.broadcasted_iota(jnp.int32, (columns, QUAD * LANES), 0)
    place = lax.broadcasted_iota(jnp.int32, (columns, QUAD * LANES), 1)
    split = (source == (place % ENTRY_SPAN) * QUAD + place // LANES).astype(jnp.float32).astype(jnp.bfloat16)
    table_base = jnp.where(lane_number() < ENTRY_SPAN, 0, ENTRY_SPAN)
    for vel_ref, target in zip(vel_refs, targets):
        for level in range(vel_ref.shape[0]):
            spread = jnp.dot(
                vel_ref[level].astype(jnp.float32).astype(jnp.bfloat16), split, preferred_element_type=jnp.float32
            ).astype(jnp.int32)
            for y in range(QUAD):
                numbers[y] = spread[:, y * LANES : (y + 1) * LANES]
            for x in range(SUB):
                for y in range(QUAD):
                    index_ref[target + level, x, y] = numbers[y, pl.ds(x, SUB, stride=SUB)] + table_base


def early_kernel(sizes, table_ref, *refs):
    groups, levels, terms = sizes
    vel_refs = refs[:-3]
    coef_ref, index_ref, numbers = refs[-3:]
    place_velocities(vel_refs, [slot * levels for slot in range(len(vel_refs))], numbers, index_ref)
    for z in range(len(vel_refs) * levels):
        for x in range(READY):
            for y in range(QUAD):
                index = index_ref[z, x, y]
                for g in range(groups):
                    for c in range(2):
                        for k in range(terms):
                            coef_ref[z, g, c, k, x, y] = lane_take(table_ref[g, c, k], index)


def image_kernel(sizes, scale, table_ref, first_ref, coef_ref, early_index_ref, *refs):
    groups, depth_count, levels, terms = sizes
    early = coef_ref.shape[0] // levels
    vel_refs = refs[: depth_count - early]
    keep_ref, send_ref, numbers, index_ref, layers, basis = refs[depth_count - early :]
    depth_pos = lax.axis_index("depth")
    depths = depth_count * levels
    columns = QUAD * ENTRY_SPAN
    masks = edge_masks()

    targets = [jnp.bitwise_xor(depth_pos, slot) * levels for slot in range(early, depth_count)]
    place_velocities(vel_refs, targets, numbers, index_ref)

    def accumulate(z, coefficients, source):
        for x in range(SUB):
            for y in range(QUAD):
                coefficient = coefficients(x, y)
                layer = None
                for g in range(groups):
                    real = imag = None
                    for k in range(terms):
                        coef_r, coef_i = coefficient(g, 0, k), coefficient(g, 1, k)
                        field_r, field_i = source[g, k, 0, x, y], source[g, k, 1, x, y]
                        if k == 0:
                            real = coef_r * field_r - coef_i * field_i
                            imag = coef_r * field_i + coef_i * field_r
                        else:
                            real = real + coef_r * field_r - coef_i * field_i
                            imag = imag + coef_r * field_i + coef_i * field_r
                    basis[g, 0, 0, x, y] = real
                    basis[g, 0, 1, x, y] = imag
                    layer = real if layer is None else layer + real
                layers[z, y, pl.ds(x, SUB, stride=SUB)] = layer * scale

    def image_of(z, source):
        slot = jnp.bitwise_xor(z // levels, depth_pos)

        @pl.when(slot < early)
        def _():
            at = slot * levels + z % levels

            def read(x, y):
                if x < READY:
                    return lambda g, c, k: coef_ref[at, g, c, k, x, y]
                index = early_index_ref[at, x, y]
                return lambda g, c, k: lane_take(table_ref[g, c, k], index)

            accumulate(z, read, source)

        @pl.when(slot >= early)
        def _():
            def look_up(x, y):
                index = index_ref[z, x, y]
                return lambda g, c, k: lane_take(table_ref[g, c, k], index)

            accumulate(z, look_up, source)

    def depth_step(z, carry):
        for g in range(groups):
            for c in range(2):
                start = [[basis[g, 0, c, x, y] for y in range(QUAD)] for x in range(SUB)]

                def put(k, x, y, value):
                    basis[g, k, c, x, y] = value

                chebyshev(start, terms, masks, put)
        image_of(z, basis)
        return carry

    image_of(0, first_ref)
    lax.fori_loop(1, depths, depth_step, 0)

    turned = lax.broadcasted_iota(jnp.int32, (LANES, columns), 0) % ENTRY_SPAN * QUAD
    wanted = lax.broadcasted_iota(jnp.int32, (LANES, columns), 1)
    joins = jnp.concatenate([(wanted == turned + y).astype(jnp.float32).astype(jnp.bfloat16) for y in range(QUAD)], axis=0)
    rows = layers.shape[2]
    chunk = math.gcd(depths, 4)

    def join(step, carry):
        rest = jnp.concatenate(
            [jnp.concatenate([layers[step * chunk + i, y] for y in range(QUAD)], axis=1) for i in range(chunk)], axis=0
        )
        whole = None
        for part in range(2):
            piece = rest.astype(jnp.bfloat16)
            rest = rest - piece.astype(jnp.float32)
            product = jnp.dot(piece, joins, preferred_element_type=jnp.float32)
            whole = product if whole is None else whole + product
        for i in range(chunk):
            z = step * chunk + i
            place = jnp.bitwise_xor(z // levels, depth_pos)
            level = z % levels

            def emit(ref):
                ref[(place // 2) * levels + level] = whole[i * rows : (i + 1) * rows]

            side = jnp.bitwise_xor(place, place // 2) % 2
            pl.when(side == 0)(functools.partial(emit, keep_ref))
            pl.when(side == 1)(functools.partial(emit, send_ref))
        return carry

    lax.fori_loop(0, depths // chunk, join, 0)


def per_device(surface, freq_slot, tap_table, vel_index):
    local_count, _, rows, columns = surface.shape
    depth_count = lax.axis_size("depth")
    freq_count = lax.axis_size("freq")
    levels = vel_index.shape[0]
    _, terms, entries, table_freqs = tap_table.shape
    count = -(-local_count // depth_count)
    groups = -(-count // PAIR)
    depths = depth_count * levels
    vmem = pl.BlockSpec(memory_space=pltpu.VMEM)
    params = pltpu.CompilerParams(vmem_limit_bytes=40 * 1024 * 1024)

    near = exchange(vel_index, "depth", 1)
    far = [exchange(vel_index, "depth", flip) for flip in range(2, depth_count, 2)]

    basis_shape = (groups, terms, 2, SUB, QUAD, SUB, LANES)
    hbm = pl.BlockSpec(memory_space=pltpu.HBM)
    table, basis, own_vel = pl.pallas_call(
        functools.partial(first_kernel, (groups, count, local_count, terms, entries)),
        out_shape=(
            jax.ShapeDtypeStruct((groups, 2, terms, SUB, LANES), jnp.float32),
            jax.ShapeDtypeStruct(basis_shape, jnp.float32),
            jax.ShapeDtypeStruct(vel_index.shape, jnp.int32),
        ),
        in_specs=[hbm] * 4,
        out_specs=(vmem, vmem, vmem),
        scratch_shapes=[
            pltpu.VMEM((count, 2, rows, columns), jnp.float32),
            pltpu.SemaphoreType.DMA((count,)),
            pltpu.VMEM((groups, 2, PAIR, 2, rows, LANES), jnp.float32),
            pltpu.SMEM((local_count,), jnp.int32),
            pltpu.VMEM((2 * terms * entries, table_freqs), jnp.float32),
            pltpu.SemaphoreType.DMA((3,)),
        ],
        compiler_params=params,
        cost_estimate=pl.CostEstimate(flops=200_000_000, bytes_accessed=16_000_000, transcendentals=0),
    )(
        *[
            pltpu.with_memory_space_constraint(array, pltpu.HBM)
            for array in (freq_slot, surface, tap_table.reshape(2 * terms * entries, table_freqs), vel_index)
        ]
    )

    vels = [own_vel, near]
    for value in far:
        value, table = lax.optimization_barrier((value, table))
        vels += [value, exchange(value, "depth", 1)]

    scale = 1.0 / math.sqrt(local_count * freq_count)
    half = jax.ShapeDtypeStruct((depths // 2, rows, columns), jnp.float32)
    early = vels[:EARLY]
    early_depths = len(early) * levels
    coefs, early_index = pl.pallas_call(
        functools.partial(early_kernel, (groups, levels, terms)),
        out_shape=(
            jax.ShapeDtypeStruct((early_depths, groups, 2, terms, READY, QUAD, SUB, LANES), jnp.float32),
            jax.ShapeDtypeStruct((early_depths, SUB, QUAD, SUB, LANES), jnp.int32),
        ),
        in_specs=[vmem] * (1 + len(early)),
        out_specs=(vmem, vmem),
        scratch_shapes=[pltpu.VMEM((QUAD, rows, LANES), jnp.int32)],
        compiler_params=params,
        cost_estimate=pl.CostEstimate(flops=200_000_000, bytes_accessed=16_000_000, transcendentals=0),
    )(table, *early)

    keep, send = pl.pallas_call(
        functools.partial(image_kernel, (groups, depth_count, levels, terms), scale),
        out_shape=(half, half),
        in_specs=[vmem] * (4 + depth_count - EARLY),
        out_specs=(vmem, vmem),
        scratch_shapes=[
            pltpu.VMEM((QUAD, rows, LANES), jnp.int32),
            pltpu.VMEM((depths, SUB, QUAD, SUB, LANES), jnp.int32),
            pltpu.VMEM((depths, QUAD, rows, LANES), jnp.float32),
            pltpu.VMEM(basis_shape, jnp.float32),
        ],
        compiler_params=params,
    )(table, basis, coefs, early_index, *vels[EARLY:])

    image = keep + exchange(send, "depth", 1)
    distance = 2
    while distance < depth_count:
        image = image.reshape((-1, 2, levels, rows, columns))
        flip = 3 if distance == 2 else distance
        image = (image[:, 0] + exchange(image[:, 1], "depth", flip)).reshape((-1, rows, columns))
        distance *= 2
    distance = 1
    while distance < freq_count:
        if distance == 1 and freq_count >= 4:
            image = image + exchange(image, "freq", 1) + (exchange(image, "freq", 2) + exchange(image, "freq", 3))
            distance = 4
        else:
            image = image + exchange(image, "freq", distance)
            distance *= 2
    return image


def solution(mesh):
    in_specs = (P("freq", None, None, None), P("freq"), P(), P("depth", None, None))
    out_specs = P("depth", None, None)
    return jax.shard_map(
        per_device, mesh=mesh, in_specs=in_specs, out_specs=out_specs, check_vma=False
    )
```

```python
import functools
import math

import jax
import jax.numpy as jnp
from jax import lax
from jax.experimental import pallas as pl
from jax.experimental.pallas import tpu as pltpu
from jax.sharding import PartitionSpec as P

SUB = 8
LANES = 128
PAIR = 2
QUAD = 4
ENTRY_SPAN = LANES // PAIR
READY = 5
EARLY = 2


def exchange(value, axis, flip):
    count = lax.axis_size(axis)
    return lax.ppermute(value, axis, [(i, i ^ flip) for i in range(count)])


def lane_take(vector, index):
    return jnp.take_along_axis(vector, index, axis=1, mode="promise_in_bounds")


def lane_number():
    return lax.broadcasted_iota(jnp.int32, (SUB, LANES), 1)


def edge_masks():
    lane = lane_number() % ENTRY_SPAN
    row = lax.broadcasted_iota(jnp.int32, (SUB, LANES), 0)
    return (
        (lane > 0).astype(jnp.float32),
        (lane < ENTRY_SPAN - 1).astype(jnp.float32),
        (row > 0).astype(jnp.float32),
        (row < SUB - 1).astype(jnp.float32),
    )


def chebyshev(start, terms, masks, put):
    left_mask, right_mask, top_mask, bottom_mask = masks
    current, sums = start, None
    for k in range(1, terms):
        lines = []
        for y in range(QUAD):
            column = [current[x][y] for x in range(SUB)]
            above = pltpu.roll(column[SUB - 1], 1, 0) * top_mask
            below = pltpu.roll(column[0], SUB - 1, 0) * bottom_mask
            lines.append([above] + column + [below])
        pairs = [lines[y][0] + lines[y][1] for y in range(QUAD)]
        following, following_sums = [], []
        for x in range(SUB):
            later = [lines[y][x + 1] + lines[y][x + 2] for y in range(QUAD)]
            line = [pairs[y] + later[y] for y in range(QUAD)]
            pairs = later
            left = pltpu.roll(line[QUAD - 1], 1, 1) * left_mask
            right = pltpu.roll(line[0], LANES - 1, 1) * right_mask
            line = [left] + line + [right]
            sides = [line[i] + line[i + 1] for i in range(QUAD + 1)]
            new, new_sums = [], []
            for y in range(QUAD):
                wide = sides[y] + sides[y + 1]
                total = 0.125 * wide if k == 1 else 0.25 * wide - sums[x][y]
                value = total - current[x][y]
                put(k, x, y, value)
                new.append(value)
                new_sums.append(total)
            following.append(new)
            following_sums.append(new_sums)
        current, sums = following, following_sums


def split_index(y):
    return (lane_number() % (LANES // QUAD)) * QUAD + y


def first_kernel(
    sizes, slot_hbm, surface_ref, tap_hbm, vel_hbm, table_ref, basis_ref, vel_ref, raw, raw_sem, halves, slot_ref, tap_ref, sems
):
    groups, count, local_count, terms, entries = sizes
    first = lax.axis_index("depth") * count
    members = [jnp.minimum(first + j, local_count - 1) for j in range(count)]
    slot_copy = pltpu.make_async_copy(slot_hbm, slot_ref, sems.at[0])
    tap_copy = pltpu.make_async_copy(tap_hbm, tap_ref, sems.at[1])
    vel_copy = pltpu.make_async_copy(vel_hbm, vel_ref, sems.at[2])
    copies = [pltpu.make_async_copy(surface_ref.at[members[j]], raw.at[j], raw_sem.at[j]) for j in range(count)]
    slot_copy.start()
    tap_copy.start()
    for copy in copies:
        copy.start()
    vel_copy.start()
    slot_copy.wait()
    tap_copy.wait()

    table_freqs = tap_ref.shape[1]
    rows = -(-count // SUB) * SUB
    freq_lane = lax.broadcasted_iota(jnp.int32, (rows, table_freqs), 1)
    freq_row = lax.broadcasted_iota(jnp.int32, (rows, table_freqs), 0)
    wanted = jnp.zeros((rows, table_freqs), jnp.int32)
    for j in range(count):
        wanted = jnp.where(freq_row == j, slot_ref[members[j]], wanted)
    picked = lax.dot_general(
        (freq_lane == wanted).astype(jnp.float32),
        tap_ref[...],
        (((1,), (1,)), ((), ())),
        precision=lax.Precision.HIGHEST,
        preferred_element_type=jnp.float32,
    )
    lane = lane_number()
    per_vector = LANES // entries
    for g in range(groups):
        for c in range(2):
            for k in range(terms):
                place = c * terms + k
                vector = place // per_vector
                whole = picked[:, vector * LANES : (vector + 1) * LANES]
                if whole.shape[1] < LANES:
                    whole = jnp.concatenate([whole, jnp.zeros((rows, LANES - whole.shape[1]), jnp.float32)], axis=1)
                sides = []
                for i in range(PAIR):
                    turn = ((place % per_vector) * entries - i * ENTRY_SPAN) % LANES
                    turned = pltpu.roll(whole, LANES - turn, 1) if turn else whole
                    j = min(g * PAIR + i, count - 1)
                    sides.append(jnp.broadcast_to(turned[j : j + 1], (SUB, LANES)))
                table_ref[g, c, k] = jnp.where(lane < ENTRY_SPAN, sides[0], sides[1])

    for copy in copies:
        copy.wait()
    masks = edge_masks()
    in_low = lane % ENTRY_SPAN < ENTRY_SPAN // 2
    for g in range(groups):
        for c in range(2):
            for i in range(PAIR):
                j = min(g * PAIR + i, count - 1)
                for h in range(2):
                    halves[g, c, i, h] = raw[j, c, :, h * LANES : (h + 1) * LANES]
    for y in range(QUAD):
        index = split_index(y)
        for g in range(groups):
            for c in range(2):
                for x in range(SUB):
                    sides = []
                    for i in range(PAIR):
                        low, high = [lane_take(halves[g, c, i, h, pl.ds(x, SUB, stride=SUB)], index) for h in range(2)]
                        side = jnp.where(in_low, low, high)
                        j = g * PAIR + i
                        if j >= count:
                            side = jnp.zeros_like(side)
                        elif count * lax.axis_size("depth") > local_count:
                            side = jnp.where(first + j < local_count, side, 0.0)
                        sides.append(side)
                    basis_ref[g, 0, c, x, y] = jnp.where(lane < ENTRY_SPAN, sides[0], sides[1])
    for g in range(groups):
        for c in range(2):
            start = [[basis_ref[g, 0, c, x, y] for y in range(QUAD)] for x in range(SUB)]

            def put(k, x, y, value):
                basis_ref[g, k, c, x, y] = value

            chebyshev(start, terms, masks, put)
    vel_copy.wait()


def place_velocities(vel_refs, targets, numbers, index_ref):
    columns = QUAD * ENTRY_SPAN
    source = lax.broadcasted_iota(jnp.int32, (columns, QUAD * LANES), 0)
    place = lax.broadcasted_iota(jnp.int32, (columns, QUAD * LANES), 1)
    split = (source == (place % ENTRY_SPAN) * QUAD + place // LANES).astype(jnp.float32).astype(jnp.bfloat16)
    table_base = jnp.where(lane_number() < ENTRY_SPAN, 0, ENTRY_SPAN)
    for vel_ref, target in zip(vel_refs, targets):
        for level in range(vel_ref.shape[0]):
            spread = jnp.dot(
                vel_ref[level].astype(jnp.float32).astype(jnp.bfloat16), split, preferred_element_type=jnp.float32
            ).astype(jnp.int32)
            for y in range(QUAD):
                numbers[y] = spread[:, y * LANES : (y + 1) * LANES]
            for x in range(SUB):
                for y in range(QUAD):
                    index_ref[target + level, x, y] = numbers[y, pl.ds(x, SUB, stride=SUB)] + table_base


def early_kernel(sizes, table_ref, *refs):
    groups, levels, terms = sizes
    vel_refs = refs[:-3]
    coef_ref, index_ref, numbers = refs[-3:]
    place_velocities(vel_refs, [slot * levels for slot in range(len(vel_refs))], numbers, index_ref)
    for z in range(len(vel_refs) * levels):
        for x in range(READY):
            for y in range(QUAD):
                index = index_ref[z, x, y]
                for g in range(groups):
                    for c in range(2):
                        for k in range(terms):
                            coef_ref[z, g, c, k, x, y] = lane_take(table_ref[g, c, k], index)


def image_kernel(sizes, scale, table_ref, first_ref, coef_ref, early_index_ref, *refs):
    groups, depth_count, levels, terms = sizes
    early = coef_ref.shape[0] // levels
    vel_refs = refs[: depth_count - early]
    keep_ref, send_ref, numbers, index_ref, layers, basis = refs[depth_count - early :]
    depth_pos = lax.axis_index("depth")
    depths = depth_count * levels
    columns = QUAD * ENTRY_SPAN
    masks = edge_masks()

    targets = [jnp.bitwise_xor(depth_pos, slot) * levels for slot in range(early, depth_count)]
    place_velocities(vel_refs, targets, numbers, index_ref)

    def accumulate(z, coefficients, source):
        for x in range(SUB):
            for y in range(QUAD):
                coefficient = coefficients(x, y)
                layer = None
                for g in range(groups):
                    real = imag = None
                    for k in range(terms):
                        coef_r, coef_i = coefficient(g, 0, k), coefficient(g, 1, k)
                        field_r, field_i = source[g, k, 0, x, y], source[g, k, 1, x, y]
                        if k == 0:
                            real = coef_r * field_r - coef_i * field_i
                            imag = coef_r * field_i + coef_i * field_r
                        else:
                            real = real + coef_r * field_r - coef_i * field_i
                            imag = imag + coef_r * field_i + coef_i * field_r
                    basis[g, 0, 0, x, y] = real
                    basis[g, 0, 1, x, y] = imag
                    layer = real if layer is None else layer + real
                layers[z, y, pl.ds(x, SUB, stride=SUB)] = layer * scale

    def image_of(z, source):
        slot = jnp.bitwise_xor(z // levels, depth_pos)

        @pl.when(slot < early)
        def _():
            at = slot * levels + z % levels

            def read(x, y):
                if x < READY:
                    return lambda g, c, k: coef_ref[at, g, c, k, x, y]
                index = early_index_ref[at, x, y]
                return lambda g, c, k: lane_take(table_ref[g, c, k], index)

            accumulate(z, read, source)

        @pl.when(slot >= early)
        def _():
            def look_up(x, y):
                index = index_ref[z, x, y]
                return lambda g, c, k: lane_take(table_ref[g, c, k], index)

            accumulate(z, look_up, source)

    def depth_step(z, carry):
        for g in range(groups):
            for c in range(2):
                start = [[basis[g, 0, c, x, y] for y in range(QUAD)] for x in range(SUB)]

                def put(k, x, y, value):
                    basis[g, k, c, x, y] = value

                chebyshev(start, terms, masks, put)
        image_of(z, basis)
        return carry

    image_of(0, first_ref)
    lax.fori_loop(1, depths, depth_step, 0)

    turned = lax.broadcasted_iota(jnp.int32, (LANES, columns), 0) % ENTRY_SPAN * QUAD
    wanted = lax.broadcasted_iota(jnp.int32, (LANES, columns), 1)
    joins = jnp.concatenate([(wanted == turned + y).astype(jnp.float32).astype(jnp.bfloat16) for y in range(QUAD)], axis=0)
    rows = layers.shape[2]
    chunk = math.gcd(depths, 4)

    def join(step, carry):
        rest = jnp.concatenate(
            [jnp.concatenate([layers[step * chunk + i, y] for y in range(QUAD)], axis=1) for i in range(chunk)], axis=0
        )
        whole = None
        for part in range(2):
            piece = rest.astype(jnp.bfloat16)
            rest = rest - piece.astype(jnp.float32)
            product = jnp.dot(piece, joins, preferred_element_type=jnp.float32)
            whole = product if whole is None else whole + product
        for i in range(chunk):
            z = step * chunk + i
            place = jnp.bitwise_xor(z // levels, depth_pos)
            level = z % levels

            def emit(ref):
                ref[(place // 2) * levels + level] = whole[i * rows : (i + 1) * rows]

            side = jnp.bitwise_xor(place, place // 2) % 2
            pl.when(side == 0)(functools.partial(emit, keep_ref))
            pl.when(side == 1)(functools.partial(emit, send_ref))
        return carry

    lax.fori_loop(0, depths // chunk, join, 0)


def per_device(surface, freq_slot, tap_table, vel_index):
    local_count, _, rows, columns = surface.shape
    depth_count = lax.axis_size("depth")
    freq_count = lax.axis_size("freq")
    levels = vel_index.shape[0]
    _, terms, entries, table_freqs = tap_table.shape
    count = -(-local_count // depth_count)
    groups = -(-count // PAIR)
    depths = depth_count * levels
    vmem = pl.BlockSpec(memory_space=pltpu.VMEM)
    params = pltpu.CompilerParams(vmem_limit_bytes=40 * 1024 * 1024)

    near = exchange(vel_index, "depth", 1)
    far = [exchange(vel_index, "depth", flip) for flip in range(2, depth_count, 2)]

    basis_shape = (groups, terms, 2, SUB, QUAD, SUB, LANES)
    hbm = pl.BlockSpec(memory_space=pltpu.HBM)
    table, basis, own_vel = pl.pallas_call(
        functools.partial(first_kernel, (groups, count, local_count, terms, entries)),
        out_shape=(
            jax.ShapeDtypeStruct((groups, 2, terms, SUB, LANES), jnp.float32),
            jax.ShapeDtypeStruct(basis_shape, jnp.float32),
            jax.ShapeDtypeStruct(vel_index.shape, jnp.int32),
        ),
        in_specs=[hbm] * 4,
        out_specs=(vmem, vmem, vmem),
        scratch_shapes=[
            pltpu.VMEM((count, 2, rows, columns), jnp.float32),
            pltpu.SemaphoreType.DMA((count,)),
            pltpu.VMEM((groups, 2, PAIR, 2, rows, LANES), jnp.float32),
            pltpu.SMEM((local_count,), jnp.int32),
            pltpu.VMEM((2 * terms * entries, table_freqs), jnp.float32),
            pltpu.SemaphoreType.DMA((3,)),
        ],
        compiler_params=params,
        cost_estimate=pl.CostEstimate(flops=200_000_000, bytes_accessed=16_000_000, transcendentals=0),
    )(
        *[
            pltpu.with_memory_space_constraint(array, pltpu.HBM)
            for array in (freq_slot, surface, tap_table.reshape(2 * terms * entries, table_freqs), vel_index)
        ]
    )

    vels = [own_vel, near]
    for value in far:
        value, table = lax.optimization_barrier((value, table))
        vels += [value, exchange(value, "depth", 1)]

    scale = 1.0 / math.sqrt(local_count * freq_count)
    half = jax.ShapeDtypeStruct((depths // 2, rows, columns), jnp.float32)
    early = vels[:EARLY]
    early_depths = len(early) * levels
    coefs, early_index = pl.pallas_call(
        functools.partial(early_kernel, (groups, levels, terms)),
        out_shape=(
            jax.ShapeDtypeStruct((early_depths, groups, 2, terms, READY, QUAD, SUB, LANES), jnp.float32),
            jax.ShapeDtypeStruct((early_depths, SUB, QUAD, SUB, LANES), jnp.int32),
        ),
        in_specs=[vmem] * (1 + len(early)),
        out_specs=(vmem, vmem),
        scratch_shapes=[pltpu.VMEM((QUAD, rows, LANES), jnp.int32)],
        compiler_params=params,
        cost_estimate=pl.CostEstimate(flops=200_000_000, bytes_accessed=16_000_000, transcendentals=0),
    )(table, *early)

    keep, send = pl.pallas_call(
        functools.partial(image_kernel, (groups, depth_count, levels, terms), scale),
        out_shape=(half, half),
        in_specs=[vmem] * (4 + depth_count - EARLY),
        out_specs=(vmem, vmem),
        scratch_shapes=[
            pltpu.VMEM((QUAD, rows, LANES), jnp.int32),
            pltpu.VMEM((depths, SUB, QUAD, SUB, LANES), jnp.int32),
            pltpu.VMEM((depths, QUAD, rows, LANES), jnp.float32),
            pltpu.VMEM(basis_shape, jnp.float32),
        ],
        compiler_params=params,
    )(table, basis, coefs, early_index, *vels[EARLY:])

    image = keep + exchange(send, "depth", 1)
    distance = 2
    while distance < depth_count:
        image = image.reshape((-1, 2, levels, rows, columns))
        flip = 3 if distance == 2 else distance
        image = (image[:, 0] + exchange(image[:, 1], "depth", flip)).reshape((-1, rows, columns))
        distance *= 2
    distance = 1
    while distance < freq_count:
        if distance == 1 and freq_count >= 4:
            image = image + exchange(image, "freq", 1) + (exchange(image, "freq", 2) + exchange(image, "freq", 3))
            distance = 4
        else:
            image = image + exchange(image, "freq", distance)
            distance *= 2
    return image


def solution(mesh):
    in_specs = (P("freq", None, None, None), P("freq"), P(), P("depth", None, None))
    out_specs = P("depth", None, None)
    return jax.shard_map(
        per_device, mesh=mesh, in_specs=in_specs, out_specs=out_specs, check_vma=False
    )
```
